256 devices in a mesh: ens: 16 (over z, y_hi), space: 16 (over x, y_lo, core).
Axes of the slice: x: 4, y: 4 (y_hi: 2, y_lo: 2; y = y_hi * 2 + y_lo), z: 8, core: 2. Of those that a mesh axis runs over, the one named last changes fastest.
Arguments:
- hidden_vectors: bfloat16 [16, 192, 720, 128], P('ens', 'space'), may hold values from -6 to 6
- target: float32 [2, 192, 720], P(None, 'space', 'ens'), may hold values from -6 to 6
- mix_weight: bfloat16 [2, 9, 128, 128], replicated, may hold values from -0.5 to 0.5
- basis_coef: bfloat16 [2, 9, 4, 3, 192], replicated, may hold values from -0.796875 to 0.796875
- rescaling_factors: float32 [2, 2, 128], replicated, may hold values from 0.1 to 1.9
- up_weight: bfloat16 [2, 128, 256], replicated, may hold values from -0.5 to 0.5
- down_weight: bfloat16 [2, 256, 128], replicated, may hold values from -0.375 to 0.375
- readout_matrix: bfloat16 [2, 128], replicated, may hold values from -0.5 to 0.5
- band_start: int32 [192], replicated, may hold values from -2 to 193, as said below
- band_width: int32 [192], replicated, may hold values from 1 to 4, as said below
Outputs:
- predicted_latents: bfloat16 [16, 192, 720, 128], P('ens', 'space')
- probabilistic_score: float32 [2, 192, 720], P(None, 'space', 'ens')
The draws below stay inside these ranges and needn't reach their ends.
Inputs may be any that keep to these rules, and one draw needn't show every extreme that they name: Every output latitude o has a band of band_width[o] rows; the first latitude's band has 4 rows and the last latitude's band one row. band_start[o] lies between o - 2 and o + 3 - band_width[o]; the first latitude's band starts at -2 and the last latitude's band ends at 193.
All inputs are finite; a program needn't handle non-finite values.
Results may differ from the reference program's by a relative error of at most 0.015.
Values may be sent and summed in bfloat16 or wider, within the bound.
A program may use at most 64 MiB of HBM per device.

```python
import jax
import jax.numpy as jnp
from jax import lax

C = 128
HID = 256
NLON = 720
K = 9
NVAR = 2
BMAX = 4
HALO = 2
LW = 3
BLOCKS = 2
NLAT = 192
MEMBERS = 16


def band_widths(key):
    lat_index = jnp.arange(NLAT, dtype=jnp.int32)
    base_width = jax.random.randint(jax.random.fold_in(key, 11), (NLAT,), 1, 3)
    widths = jnp.maximum(base_width, BMAX - lat_index)
    return jnp.where(lat_index == NLAT - 1, 1, widths).astype(jnp.int32)


def draw_band_width(key, part):
    return band_widths(key)


def draw_band_start(key, part):
    widths = band_widths(key)
    key = jax.random.fold_in(key, 5)
    lat_index = jnp.arange(NLAT, dtype=jnp.int32)
    start_shift = jax.random.randint(key, (NLAT,), 0, 2 * HALO + 2 - widths)
    start_shift = jnp.where(lat_index == 0, 0, start_shift)
    start_shift = jnp.where(lat_index == NLAT - 1, 2 * HALO + 1 - widths, start_shift)
    return (lat_index - HALO + start_shift).astype(jnp.int32)


def level_of(own_key, dims, shards, low, high):
    loudness = 1.0
    for axis_at, blocks in shards:
        steps = jax.random.uniform(jax.random.fold_in(jax.random.fold_in(own_key, 6), axis_at), (blocks,), jnp.float32, low / len(shards), high / len(shards))
        loudness = loudness * jnp.repeat(jnp.exp(steps), dims[axis_at] // blocks).reshape((-1,) + (1,) * (len(dims) - 1 - axis_at))
    return loudness


def normal_values(stream_key, shape, scale, most, pieces=(), kind=jnp.bfloat16):
    drawn = scale * jax.random.normal(stream_key, shape, jnp.float32)
    if pieces:
        drawn = drawn * level_of(stream_key, shape, pieces, -0.22, 0.18)
    return jnp.clip(drawn, -most, most).astype(kind)


def setup_inputs(seed: int = 0) -> dict:
    seeds = jax.random.split(jax.random.key(seed), 11)
    return {
        "hidden_vectors": normal_values(seeds[0], (MEMBERS, NLAT, NLON, C), 1.0, 6.0, ((0, 16), (1, 16))),
        "target": normal_values(seeds[1], (NVAR, NLAT, NLON), 1.0, 6.0, ((1, 16), (2, 16)), jnp.float32),
        "mix_weight": normal_values(seeds[2], (BLOCKS, K, C, C), C ** -0.5, 0.5),
        "basis_coef": normal_values(seeds[3], (BLOCKS, K, BMAX, LW, NLAT), 0.13, 0.796875),
        "rescaling_factors": jnp.clip(1.0 + 0.18 * jax.random.normal(seeds[4], (BLOCKS, 2, C), jnp.float32), 0.1, 1.9),
        "up_weight": normal_values(seeds[5], (BLOCKS, C, HID), C ** -0.5, 0.5),
        "down_weight": normal_values(seeds[6], (BLOCKS, HID, C), HID ** -0.5, 0.375),
        "readout_matrix": normal_values(seeds[7], (NVAR, C), C ** -0.5, 0.5),
        "band_start": draw_band_start(jax.random.fold_in(seeds[10], 71), 0),
        "band_width": draw_band_width(jax.random.fold_in(seeds[10], 71), 0),
    }


def normalize(values, row_gain):
    widened = values.astype(jnp.float32)
    inv_scale = lax.rsqrt(lax.optimization_barrier(jnp.mean(widened * widened, axis=-1, keepdims=True)) + 1e-06)
    return (widened * inv_scale * row_gain).astype(jnp.bfloat16)

def wrap_longitude(grid_field):
    radius = LW // 2
    return jnp.concatenate([grid_field[:, -radius:], grid_field, grid_field[:, :radius]], axis=1)

def band_matrix(coef, rel_start, widths):
    offsets = jnp.arange(BMAX, dtype=jnp.int32)
    window = jnp.arange(2 * HALO + 1, dtype=jnp.int32)
    inside = offsets[:, None, None] < widths[None, :, None]
    placed_field = window[None, None, :] == rel_start[None, :, None] + offsets[:, None, None]
    select = jnp.where(inside & placed_field, 1.0, 0.0).astype(jnp.float32)
    return jnp.einsum('kqlo,qor->klor', coef.astype(jnp.float32), select).astype(jnp.bfloat16)

def disco_rows(padded, bands, mixing_weight):
    row_count = bands.shape[2]
    lon_count = padded.shape[1] - (LW - 1)
    window_rows = 2 * HALO + 1

    def one_row(row):
        window = lax.dynamic_slice_in_dim(padded, row, window_rows, 0)
        piled_arrays = jnp.concatenate([window[:, shift:shift + lon_count].reshape(window_rows, -1) for shift in range(LW)], axis=0)
        row_weights = lax.dynamic_index_in_dim(bands, row, 2, keepdims=False).reshape(K, -1)
        gathered = jnp.dot(row_weights, piled_arrays, preferred_element_type=jnp.float32).astype(jnp.bfloat16)
        gathered = gathered.reshape(K, lon_count, -1)
        return jnp.einsum('kjc,kcd->jd', gathered.astype(jnp.float32), mixing_weight.astype(jnp.float32))
    return lax.map(one_row, jnp.arange(row_count, dtype=jnp.int32))

def block_tail(present_state, conv_sum, row_gain, up_matrix, down_matrix):
    carried_state = (present_state.astype(jnp.float32) + conv_sum).astype(jnp.bfloat16)
    normed = normalize(carried_state, row_gain)
    channels = normed.shape[-1]
    hidden = jax.nn.gelu(jnp.dot(normed.reshape(-1, channels), up_matrix, preferred_element_type=jnp.float32), approximate=False).astype(jnp.bfloat16)
    output = jnp.dot(hidden, down_matrix, preferred_element_type=jnp.float32).reshape(carried_state.shape)
    return (carried_state.astype(jnp.float32) + output).astype(jnp.bfloat16)

def reference(hidden_vectors, target, mix_weight, basis_coef, rescaling_factors, up_weight, down_weight, readout_matrix, band_start, band_width):
    rel_start = (band_start - jnp.arange(NLAT, dtype=jnp.int32) + HALO).astype(jnp.int32)

    def advance_once(member):
        present_state = member
        for block_index in range(BLOCKS):
            normed = normalize(present_state, rescaling_factors[block_index, 0])
            padded = jnp.pad(wrap_longitude(normed), ((HALO, HALO), (0, 0), (0, 0)))
            bands = band_matrix(basis_coef[block_index], rel_start, band_width)
            conv_sum = disco_rows(padded, bands, mix_weight[block_index])
            present_state = block_tail(present_state, conv_sum, rescaling_factors[block_index, 1], up_weight[block_index], down_weight[block_index])
        return present_state
    predicted_latents = lax.map(advance_once, hidden_vectors)
    lowest_level_prediction = jnp.einsum('uzgm,wm->uwzg', predicted_latents.astype(jnp.float32), readout_matrix.astype(jnp.float32))
    skill_term = lax.optimization_barrier(jnp.mean(jnp.abs(lowest_level_prediction - target[None]), axis=0))

    def pair_sum(member_surface_field):
        return lax.optimization_barrier(jnp.sum(jnp.abs(member_surface_field[None] - lowest_level_prediction), axis=0))
    spread_sum = lax.optimization_barrier(jnp.sum(lax.map(pair_sum, lowest_level_prediction), axis=0))
    probabilistic_score = skill_term - spread_sum / (2.0 * MEMBERS * (MEMBERS - 1))
    return (predicted_latents, probabilistic_score)
```

```python
import jax
import jax.numpy as jnp
from jax import lax
from jax.experimental import pallas as pl
from jax.experimental.pallas import tpu as pltpu
from jax.sharding import PartitionSpec as P

K = 9
BMAX = 4
HALO = 2
LW = 3
BLOCKS = 2
ROWS = 12
LON = 720
PAIRS = 368
C = 128
STEP = 80
PARTS = ((0, 192), (192, 176))
f32 = jnp.float32
bf16 = jnp.bfloat16


def unit(v, gain):
    return v * lax.rsqrt(jnp.mean(v * v, axis=-1, keepdims=True) + 1e-6) * gain


def prep_row(x, gain, a, s, nrm, raw):
    for t in range(0, LON, STEP):
        v = x[pl.ds(t, STEP), :].astype(f32)
        nrm[pl.ds(8 + t, STEP), :] = unit(v, gain)
        if s is not None:
            raw[pl.ds(t, STEP), :] = v
    nrm[7:8, :] = nrm[727:728, :]
    nrm[728:729, :] = nrm[8:9, :]
    for j in range(4):
        a[:, j * C : (j + 1) * C] = nrm[pl.ds(7 + j, PAIRS, stride=2), :].astype(bf16)
    if s is not None:
        for j in range(2):
            s[:, j * C : (j + 1) * C] = raw[pl.ds(j, PAIRS, stride=2), :].astype(bf16)


def make_taps(band, mix, mx, wf, taps):
    mx[...] = jnp.zeros_like(mx)
    for k in range(K):
        mx[pl.ds(k, C, stride=16), :] = mix[k].astype(f32)
    coef = band[...]

    def channels(i, carry):
        for u in range(4):
            c = i * 4 + u
            rhs = jnp.concatenate(
                [mx[pl.ds(c * 32, 16), :], mx[pl.ds(c * 32 + 16, 16), :]], axis=1
            ).astype(bf16)
            out = jnp.dot(coef, rhs, preferred_element_type=f32)
            wf[pl.ds(c * 288, 144), :] = out[:, :C]
            wf[pl.ds(c * 288 + 144, 144), :] = out[:, C:]
        return carry

    lax.fori_loop(0, 16, channels, 0)

    def place(i, carry):
        for l in range(LW):
            w = wf[pl.ds(i * LW + l, C, stride=144), :].astype(bf16)
            taps[i, l * C : (l + 1) * C, 0:C] = w
            taps[i, (l + 1) * C : (l + 2) * C, C : 2 * C] = w
        taps[i, 3 * C : 4 * C, 0:C] = jnp.zeros((C, C), bf16)
        taps[i, 0:C, C : 2 * C] = jnp.zeros((C, C), bf16)
        return carry

    lax.fori_loop(0, ROWS * BMAX, place, 0)


def conv_row(o, start, a, s, taps, car):
    rows = [jnp.clip(start[o] + q, 0, ROWS + 2 * HALO - 1) for q in range(BMAX)]
    for p, n in PARTS:
        acc = jnp.dot(a[rows[0], pl.ds(p, n), :], taps[o * BMAX], preferred_element_type=f32)
        for q in range(1, BMAX):
            acc += jnp.dot(
                a[rows[q], pl.ds(p, n), :], taps[o * BMAX + q], preferred_element_type=f32
            )
        car[pl.ds(p, n), :] = (s[o, pl.ds(p, n), :].astype(f32) + acc).astype(bf16).astype(f32)


def mlp_row(gain, up, down, car, emit):
    for p, n in PARTS:
        rest = jnp.concatenate([car[pl.ds(p, n), :C], car[pl.ds(p, n), C:]], axis=0)
        h = jnp.dot(unit(rest, gain).astype(bf16), up, preferred_element_type=f32)
        h = (0.5 * h * (1.0 + lax.erf(h * 0.7071067811865476))).astype(bf16)
        y = rest + jnp.dot(h, down, preferred_element_type=f32)
        emit(p, n, y[:n], y[n:])


def block_kernel(
    start, x, before, after, band, mix, gains, up, down, out, a, s, taps, nrm, raw, fin, mx, wf, car
):
    make_taps(band, mix, mx, wf, taps)
    gain = gains[0:1]

    def prep(i, carry):
        prep_row(x.at[i], gain, a.at[i + HALO], s.at[i], nrm, raw)
        return carry

    lax.fori_loop(0, ROWS, prep, 0)
    for i in range(HALO):
        prep_row(before.at[i], gain, a.at[i], None, nrm, raw)
        prep_row(after.at[i], gain, a.at[ROWS + HALO + i], None, nrm, raw)
    gain2 = gains[1:2]
    up_matrix, down_matrix = up[...], down[...]

    def row(o, carry):
        def emit(p, n, even, odd):
            fin[pl.ds(2 * p, n, stride=2), :] = even
            fin[pl.ds(2 * p + 1, n, stride=2), :] = odd

        conv_row(o, start, a, s, taps, car)
        mlp_row(gain2, up_matrix, down_matrix, car, emit)
        out[o] = fin[0:LON, :].astype(bf16)
        return carry

    lax.fori_loop(0, ROWS, row, 0)


def block(start, x, before, after, band, mix, gains, up, down):
    vmem = pl.BlockSpec(memory_space=pltpu.VMEM)
    return pl.pallas_call(
        block_kernel,
        out_shape=jax.ShapeDtypeStruct(x.shape, bf16),
        in_specs=[pl.BlockSpec(memory_space=pltpu.SMEM)] + [vmem] * 8,
        out_specs=vmem,
        scratch_shapes=[
            pltpu.VMEM((ROWS + 2 * HALO, PAIRS, 4 * C), bf16),
            pltpu.VMEM((ROWS, PAIRS, 2 * C), bf16),
            pltpu.VMEM((ROWS * BMAX, 4 * C, 2 * C), bf16),
            pltpu.VMEM((752, C), f32),
            pltpu.VMEM((2 * PAIRS, C), f32),
            pltpu.VMEM((2 * PAIRS, C), f32),
            pltpu.VMEM((16 * C, C), f32),
            pltpu.VMEM((144 * C, C), f32),
            pltpu.VMEM((PAIRS, 2 * C), f32),
        ],
        compiler_params=pltpu.CompilerParams(vmem_limit_bytes=56 * 2**20),
    )(start, x, before, after, band, mix, gains, up, down)


def band_taps(basis_coef, local_width, row_first):
    coef = lax.dynamic_slice_in_dim(basis_coef, row_first, ROWS, axis=4)
    inside = jnp.arange(BMAX, dtype=jnp.int32)[:, None] < local_width[None, :]
    coef = jnp.where(inside[None, None, :, None, :], coef, jnp.zeros_like(coef))
    coef = coef.transpose(0, 4, 2, 3, 1).reshape(BLOCKS, ROWS * BMAX * LW, K)
    return jnp.pad(coef, ((0, 0), (0, 0), (0, 16 - K)))


def body(
    hidden_vectors,
    target,
    mix_weight,
    basis_coef,
    rescaling_factors,
    up_weight,
    down_weight,
    readout_matrix,
    band_start,
    band_width,
):
    row_first = lax.axis_index("space") * ROWS
    local_start = lax.dynamic_slice_in_dim(band_start, row_first, ROWS)
    local_width = lax.dynamic_slice_in_dim(band_width, row_first, ROWS)
    start = local_start - row_first + HALO
    bands = band_taps(basis_coef, local_width, row_first)
    peers = lax.axis_size("space")
    forward = [(i, i + 1) for i in range(peers - 1)]
    backward = [(j, i) for i, j in forward]
    x = hidden_vectors[0]
    for b in range(BLOCKS):
        before = lax.ppermute(x[ROWS - HALO :], "space", forward)
        after = lax.ppermute(x[:HALO], "space", backward)
        x = block(
            start,
            x,
            before,
            after,
            bands[b],
            mix_weight[b],
            rescaling_factors[b],
            up_weight[b],
            down_weight[b],
        )
    state = x[None]
    surface = jnp.einsum("uzgm,wm->uwzg", state, readout_matrix, preferred_element_type=f32)
    lon_cols = target.shape[2]
    everyone = lax.all_gather(surface.astype(bf16), "ens", axis=0, tiled=True).astype(f32)
    members = lax.dynamic_slice_in_dim(
        everyone, lax.axis_index("ens") * lon_cols, lon_cols, axis=3
    )
    count = members.shape[0]
    skill = jnp.mean(jnp.abs(members - target[None]), axis=0)
    spread = jnp.sum(jnp.abs(members[:, None] - members[None]), axis=(0, 1))
    return (state, skill - spread / (2.0 * count * (count - 1)))


def solution(mesh):
    in_specs = (P("ens", "space", None, None), P(None, "space", "ens")) + (P(),) * 8
    out_specs = (P("ens", "space", None, None), P(None, "space", "ens"))
    return jax.shard_map(body, mesh=mesh, in_specs=in_specs, out_specs=out_specs, check_vma=False)
```

```python
import jax
import jax.numpy as jnp
from jax import lax
from jax.experimental import pallas as pl
from jax.experimental.pallas import tpu as pltpu
from jax.sharding import PartitionSpec as P

K = 9
BMAX = 4
HALO = 2
LW = 3
BLOCKS = 2
ROWS = 12
LON = 720
PAIRS = 368
C = 128
STEP = 80
PARTS = ((0, 192), (192, 176))
f32 = jnp.float32
bf16 = jnp.bfloat16
MESH = pl.DeviceIdType.MESH


def unit(v, gain):
    return v * lax.rsqrt(jnp.mean(v * v, axis=-1, keepdims=True) + 1e-6) * gain


def prep_row(x, gain, a, s, nrm, raw):
    for t in range(0, LON, STEP):
        v = x[pl.ds(t, STEP), :].astype(f32)
        nrm[pl.ds(8 + t, STEP), :] = unit(v, gain)
        if s is not None:
            raw[pl.ds(t, STEP), :] = v
    nrm[7:8, :] = nrm[727:728, :]
    nrm[728:729, :] = nrm[8:9, :]
    for j in range(4):
        a[:, j * C : (j + 1) * C] = nrm[pl.ds(7 + j, PAIRS, stride=2), :].astype(bf16)
    if s is not None:
        for j in range(2):
            s[:, j * C : (j + 1) * C] = raw[pl.ds(j, PAIRS, stride=2), :].astype(bf16)


def band_rows(b, me, basis, width, cf, bnd):
    lat = jax.lax.broadcasted_iota(jnp.int32, (16, 192), 1)
    own = jax.lax.broadcasted_iota(jnp.int32, (16, 192), 0)
    pick = jnp.where((lat == own + me * ROWS) & (own < ROWS), 1.0, 0.0).astype(bf16)
    row = jax.lax.broadcasted_iota(jnp.int32, (16, 16), 0)
    widths = jnp.zeros((16, 16), jnp.int32)
    for o in range(ROWS):
        widths = jnp.where(row == o, width[me * ROWS + o], widths)
    for k in range(K):
        for q in range(BMAX):
            v = basis[b, k, q].astype(f32)
            for l in range(LW):
                at = (q * LW + l) * 16 + k
                cf[at : at + 1, 0:192] = v[l : l + 1]
    for q in range(BMAX):
        for l in range(LW):
            at = q * LW + l
            part = lax.dot_general(
                pick,
                cf[at * 16 : at * 16 + 16, 0:192].astype(bf16),
                (((1,), (1,)), ((), ())),
                preferred_element_type=f32,
            )
            part = jnp.where(widths > q, part, 0.0)
            bnd[at * ROWS : at * ROWS + ROWS, 0:16] = part[:ROWS]


def make_taps(b, mix, mx, wf, bnd, taps):
    for k in range(K):
        mx[pl.ds(k, C, stride=16), :] = mix[b, k].astype(f32)
    coef = bnd[0:144, 0:16].astype(bf16)

    def channels(i, carry):
        for u in range(4):
            c = i * 4 + u
            rhs = jnp.concatenate(
                [mx[pl.ds(c * 32, 16), :], mx[pl.ds(c * 32 + 16, 16), :]], axis=1
            ).astype(bf16)
            out = jnp.dot(coef, rhs, preferred_element_type=f32)
            wf[pl.ds(c * 288, 144), :] = out[:, :C]
            wf[pl.ds(c * 288 + 144, 144), :] = out[:, C:]
        return carry

    lax.fori_loop(0, 16, channels, 0)

    def place(o, carry):
        for q in range(BMAX):
            i = o * BMAX + q
            for l in range(LW):
                w = wf[pl.ds((q * LW + l) * ROWS + o, C, stride=144), :].astype(bf16)
                taps[i, l * C : (l + 1) * C, 0:C] = w
                taps[i, (l + 1) * C : (l + 2) * C, C : 2 * C] = w
        return carry

    lax.fori_loop(0, ROWS, place, 0)


def prep_pairs(s, gain, a, even, odd):
    for p, n in PARTS:
        e = unit(s[pl.ds(p, n), 0:C].astype(f32), gain)
        o = unit(s[pl.ds(p, n), C : 2 * C].astype(f32), gain)
        a[pl.ds(p, n), C : 2 * C] = e.astype(bf16)
        a[pl.ds(p, n), 2 * C : 3 * C] = o.astype(bf16)
        even[pl.ds(8 + p, n), :] = e
        odd[pl.ds(8 + p, n), :] = o
    odd[7:8, :] = odd[367:368, :]
    even[368:369, :] = even[8:9, :]
    a[:, 0:C] = odd[7 : 7 + PAIRS, :].astype(bf16)
    a[:, 3 * C : 4 * C] = even[9 : 9 + PAIRS, :].astype(bf16)


def conv_row(o, start, first, a, s, taps, car):
    base = start[first + o] - first + HALO
    rows = [jnp.clip(base + q, 0, ROWS + 2 * HALO - 1) for q in range(BMAX)]
    for p, n in PARTS:
        acc = jnp.dot(a[rows[0], pl.ds(p, n), :], taps[o * BMAX], preferred_element_type=f32)
        for q in range(1, BMAX):
            acc += jnp.dot(
                a[rows[q], pl.ds(p, n), :], taps[o * BMAX + q], preferred_element_type=f32
            )
        car[pl.ds(p, n), :] = (s[o, pl.ds(p, n), :].astype(f32) + acc).astype(bf16).astype(f32)


def mlp_row(gain, up, down, car, emit):
    for p, n in PARTS:
        rest = jnp.concatenate([car[pl.ds(p, n), :C], car[pl.ds(p, n), C:]], axis=0)
        h = jnp.dot(unit(rest, gain).astype(bf16), up, preferred_element_type=f32)
        h = (0.5 * h * (1.0 + lax.erf(h * 0.7071067811865476))).astype(bf16)
        y = rest + jnp.dot(h, down, preferred_element_type=f32)
        emit(p, n, y[:n], y[n:])


def both(first, second):
    lane = jax.lax.broadcasted_iota(jnp.int32, first.shape, 1)
    return jnp.where(lane < 64, first, pltpu.roll(second, 64, 1))


def step_kernel(
    start, width, x, target, mix, basis, gains, up, down, readout,
    out, score,
    xv, ov, a, s, taps, nrm, raw, fin, mx, wf, car, cf, bnd, even, odd,
    halo0, halo1, surf, tgt, snd, rcv,
    x_sem, out_sem, send_sem, recv_sem, ens_send, ens_recv,
):
    me = lax.axis_index("space")
    ens = lax.axis_index("ens")
    members = rcv.shape[0]
    last = lax.axis_size("space") - 1
    barrier = pltpu.get_barrier_semaphore()
    for step in range(1, members):
        pl.semaphore_signal(
            barrier, inc=1, device_id={"ens": lax.rem(ens + step, members)}, device_id_type=MESH
        )

    @pl.when(me > 0)
    def _():
        pl.semaphore_signal(barrier, inc=1, device_id={"space": me - 1}, device_id_type=MESH)

    @pl.when(me < last)
    def _():
        pl.semaphore_signal(barrier, inc=1, device_id={"space": me + 1}, device_id_type=MESH)

    x_copy = pltpu.make_async_copy(x.at[0], xv, x_sem)
    x_copy.start()
    mx[...] = jnp.zeros_like(mx)
    cf[...] = jnp.zeros_like(cf)

    def clear(i, carry):
        taps[i, 3 * C : 4 * C, 0:C] = jnp.zeros((C, C), bf16)
        taps[i, 0:C, C : 2 * C] = jnp.zeros((C, C), bf16)
        return carry

    lax.fori_loop(0, ROWS * BMAX, clear, 0)
    for i in range(HALO):
        a[i] = jnp.zeros((PAIRS, 4 * C), bf16)
        a[ROWS + HALO + i] = jnp.zeros((PAIRS, 4 * C), bf16)
    band_rows(0, me, basis, width, cf, bnd)
    make_taps(0, mix, mx, wf, bnd, taps)

    middle = (me > 0) & (me < last)

    @pl.when(middle)
    def _():
        pl.semaphore_wait(barrier, members + 1)

    @pl.when(jnp.logical_not(middle))
    def _():
        pl.semaphore_wait(barrier, members)

    def forward(b):
        source, landing = (x.at[0], halo0) if b == 0 else (s, halo1)
        return pltpu.make_async_remote_copy(
            src_ref=source.at[pl.ds(ROWS - HALO, HALO)],
            dst_ref=landing.at[pl.ds(0, HALO)],
            send_sem=send_sem.at[b, 0],
            recv_sem=recv_sem.at[b, 0],
            device_id={"space": me + 1},
            device_id_type=MESH,
        )

    def backward(b):
        source, landing = (x.at[0], halo0) if b == 0 else (s, halo1)
        return pltpu.make_async_remote_copy(
            src_ref=source.at[pl.ds(0, HALO)],
            dst_ref=landing.at[pl.ds(HALO, HALO)],
            send_sem=send_sem.at[b, 1],
            recv_sem=recv_sem.at[b, 1],
            device_id={"space": me - 1},
            device_id_type=MESH,
        )

    def send_forward(b):
        @pl.when(me < last)
        def _():
            forward(b).start()

    def send_backward(b):
        @pl.when(me > 0)
        def _():
            backward(b).start()

    send_forward(0)
    send_backward(0)
    first = me * ROWS

    def halo_rows(b, side):
        def fill(i, carry):
            at = side * HALO + i
            row = a.at[side * (ROWS + HALO) + i]
            if b == 0:
                prep_row(halo0.at[at], gains[0, 0:1], row, None, nrm, raw)
            else:
                prep_pairs(halo1.at[at], gains[1, 0:1], row, even, odd)
            return carry

        def empty():
            for i in range(HALO):
                a[side * (ROWS + HALO) + i] = jnp.zeros((PAIRS, 4 * C), bf16)

        has = me > 0 if side == 0 else me < last

        @pl.when(has)
        def _():
            (forward(b) if side == 0 else backward(b)).wait_recv()
            lax.fori_loop(0, HALO, fill, 0)

        @pl.when(jnp.logical_not(has))
        def _():
            empty()

    lead = jnp.concatenate([readout[...].astype(f32), jnp.zeros((14, C), f32)], axis=0).astype(bf16)

    def rows(b, low, high):
        gain2 = gains[b, 1:2]
        up_matrix, down_matrix = up[b], down[b]

        def row(o, carry):
            def emit(p, n, e, d):
                if b == 0:
                    s[o, pl.ds(p, n), 0:C] = e.astype(bf16)
                    s[o, pl.ds(p, n), C : 2 * C] = d.astype(bf16)
                else:
                    fin[pl.ds(2 * p, n, stride=2), :] = e
                    fin[pl.ds(2 * p + 1, n, stride=2), :] = d

            conv_row(o, start, first, a, s, taps, car)
            mlp_row(gain2, up_matrix, down_matrix, car, emit)
            if b == 1:
                state = fin[0:LON, :].astype(bf16)
                ov[o] = state
                pltpu.make_async_copy(ov.at[o], out.at[0, o], out_sem.at[o]).start()
                seen = lax.dot_general(
                    lead, state, (((1,), (1,)), ((), ())), preferred_element_type=f32
                )
                surf[pl.ds(o, 1), 0:LON] = seen[0:1]
                surf[pl.ds(16 + o, 1), 0:LON] = seen[1:2]
            return carry

        lax.fori_loop(low, high, row, 0)

    x_copy.wait()

    def prep0(i, carry):
        prep_row(xv.at[i], gains[0, 0:1], a.at[i + HALO], s.at[i], nrm, raw)
        return carry

    lax.fori_loop(0, ROWS, prep0, 0)
    rows(0, HALO, ROWS - HALO)
    halo_rows(0, 0)
    rows(0, 0, HALO)
    send_backward(1)
    halo_rows(0, 1)
    rows(0, ROWS - HALO, ROWS)
    send_forward(1)

    band_rows(1, me, basis, width, cf, bnd)
    make_taps(1, mix, mx, wf, bnd, taps)

    def prep1(i, carry):
        prep_pairs(s.at[i], gains[1, 0:1], a.at[i + HALO], even, odd)
        return carry

    lax.fori_loop(0, ROWS, prep1, 0)
    rows(1, HALO, ROWS - HALO)
    halo_rows(1, 0)
    rows(1, 0, HALO)
    halo_rows(1, 1)
    rows(1, ROWS - HALO, ROWS)

    cols = target.shape[2]
    for e in range(members):
        base = e * cols // 128 * 128
        turn = (256 - (e * cols - base)) % 256
        top = pltpu.roll(surf[0:16, base : base + 256], turn, 1)[:, 0:128]
        low = pltpu.roll(surf[16:32, base : base + 256], turn, 1)[:, 0:128]
        snd[e] = both(top, low).astype(bf16)
    rcv[ens] = snd[ens]

    def deal(step):
        peer = lax.rem(ens + step, members)
        return pltpu.make_async_remote_copy(
            src_ref=snd.at[peer],
            dst_ref=rcv.at[ens],
            send_sem=ens_send.at[step],
            recv_sem=ens_recv.at[ens],
            device_id={"ens": peer},
            device_id_type=MESH,
        )

    for step in range(1, members):
        deal(step).start()
    for v in range(2):
        tgt[v, 0:ROWS, 0:cols] = target[v]
    for step in range(1, members):
        peer = lax.rem(ens + step, members)
        pltpu.make_async_remote_copy(
            src_ref=snd.at[peer],
            dst_ref=rcv.at[peer],
            send_sem=ens_send.at[step],
            recv_sem=ens_recv.at[peer],
            device_id={"ens": peer},
            device_id_type=MESH,
        ).wait_recv()
    aim = both(tgt[0], tgt[1])
    field = [rcv[m].astype(f32) for m in range(members)]
    skill = sum(jnp.abs(f - aim) for f in field) * (1.0 / members)
    spread = jnp.zeros_like(aim)
    for m in range(members):
        for n in range(m):
            spread = spread + jnp.abs(field[m] - field[n])
    fair = skill - spread * (1.0 / (members * (members - 1)))
    score[0] = fair[0:ROWS, 0:cols]
    score[1] = pltpu.roll(fair, 64, 1)[0:ROWS, 0:cols]

    for step in range(1, members):
        deal(step).wait_send()
    for b in range(BLOCKS):

        @pl.when(me < last)
        def _():
            forward(b).wait_send()

        @pl.when(me > 0)
        def _():
            backward(b).wait_send()

    def finish(o, carry):
        pltpu.make_async_copy(ov.at[o], out.at[0, o], out_sem.at[o]).wait()
        return carry

    lax.fori_loop(0, ROWS, finish, 0)


def body(
    hidden_vectors, target, mix_weight, basis_coef, rescaling_factors,
    up_weight, down_weight, readout_matrix, band_start, band_width,
):
    members = lax.axis_size("ens")
    vmem = pl.BlockSpec(memory_space=pltpu.VMEM)
    smem = pl.BlockSpec(memory_space=pltpu.SMEM)
    return pl.pallas_call(
        step_kernel,
        out_shape=(
            jax.ShapeDtypeStruct(hidden_vectors.shape, bf16),
            jax.ShapeDtypeStruct(target.shape, f32),
        ),
        in_specs=[smem, smem, pl.BlockSpec(memory_space=pl.ANY)] + [vmem] * 7,
        out_specs=(pl.BlockSpec(memory_space=pl.ANY), vmem),
        scratch_shapes=[
            pltpu.VMEM((ROWS, LON, C), bf16),
            pltpu.VMEM((ROWS, LON, C), bf16),
            pltpu.VMEM((ROWS + 2 * HALO, PAIRS, 4 * C), bf16),
            pltpu.VMEM((ROWS, PAIRS, 2 * C), bf16),
            pltpu.VMEM((ROWS * BMAX, 4 * C, 2 * C), bf16),
            pltpu.VMEM((752, C), f32),
            pltpu.VMEM((2 * PAIRS, C), f32),
            pltpu.VMEM((2 * PAIRS, C), f32),
            pltpu.VMEM((16 * C, C), f32),
            pltpu.VMEM((144 * C, C), f32),
            pltpu.VMEM((PAIRS, 2 * C), f32),
            pltpu.VMEM((192, 256), f32),
            pltpu.VMEM((144, C), f32),
            pltpu.VMEM((384, C), f32),
            pltpu.VMEM((384, C), f32),
            pltpu.VMEM((2 * HALO, LON, C), bf16),
            pltpu.VMEM((2 * HALO, PAIRS, 2 * C), bf16),
            pltpu.VMEM((32, 896), f32),
            pltpu.VMEM((2, 16, 128), f32),
            pltpu.VMEM((members, 16, 128), bf16),
            pltpu.VMEM((members, 16, 128), bf16),
            pltpu.SemaphoreType.DMA,
            pltpu.SemaphoreType.DMA((ROWS,)),
            pltpu.SemaphoreType.DMA((2, 2)),
            pltpu.SemaphoreType.DMA((2, 2)),
            pltpu.SemaphoreType.DMA((members,)),
            pltpu.SemaphoreType.DMA((members,)),
        ],
        compiler_params=pltpu.CompilerParams(
            vmem_limit_bytes=56 * 2**20, collective_id=0, has_side_effects=True
        ),
    )(
        band_start, band_width, hidden_vectors, target, mix_weight, basis_coef,
        rescaling_factors, up_weight, down_weight, readout_matrix,
    )


def solution(mesh):
    in_specs = (P("ens", "space", None, None), P(None, "space", "ens")) + (P(),) * 8
    out_specs = (P("ens", "space", None, None), P(None, "space", "ens"))
    return jax.shard_map(body, mesh=mesh, in_specs=in_specs, out_specs=out_specs, check_vma=False)
```

```python
import jax
import jax.numpy as jnp
from jax import lax
from jax.experimental import pallas as pl
from jax.experimental.pallas import tpu as pltpu
from jax.sharding import PartitionSpec as P

K = 9
BMAX = 4
HALO = 2
LW = 3
BLOCKS = 2
ROWS = 12
LON = 720
PAIRS = 368
C = 128
STEP = 80
PARTS = ((0, 192), (192, 176))
f32 = jnp.float32
bf16 = jnp.bfloat16
MESH = pl.DeviceIdType.MESH


def unit(v, gain):
    return v * lax.rsqrt(jnp.mean(v * v, axis=-1, keepdims=True) + 1e-6) * gain


def prep_row(x, gain, a, s, nrm, raw):
    for t in range(0, LON, STEP):
        v = x[pl.ds(t, STEP), :].astype(f32)
        nrm[pl.ds(8 + t, STEP), :] = unit(v, gain)
        if s is not None:
            raw[pl.ds(t, STEP), :] = v
    nrm[7:8, :] = nrm[727:728, :]
    nrm[728:729, :] = nrm[8:9, :]
    for j in range(4):
        a[:, j * C : (j + 1) * C] = nrm[pl.ds(7 + j, PAIRS, stride=2), :].astype(bf16)
    if s is not None:
        for j in range(2):
            s[:, j * C : (j + 1) * C] = raw[pl.ds(j, PAIRS, stride=2), :].astype(bf16)


def band_rows(b, me, basis, width, cf, bnd):
    lat = jax.lax.broadcasted_iota(jnp.int32, (16, 192), 1)
    own = jax.lax.broadcasted_iota(jnp.int32, (16, 192), 0)
    pick = jnp.where((lat == own + me * ROWS) & (own < ROWS), 1.0, 0.0).astype(bf16)
    row = jax.lax.broadcasted_iota(jnp.int32, (16, 16), 0)
    widths = jnp.zeros((16, 16), jnp.int32)
    for o in range(ROWS):
        widths = jnp.where(row == o, width[me * ROWS + o], widths)
    for k in range(K):
        for l in range(LW):
            v = basis[b, k, l].astype(f32)
            for q in range(BMAX):
                at = (q * LW + l) * 16 + k
                cf[at : at + 1, 0:192] = v[q : q + 1]
    for q in range(BMAX):
        for l in range(LW):
            at = q * LW + l
            part = lax.dot_general(
                pick,
                cf[at * 16 : at * 16 + 16, 0:192].astype(bf16),
                (((1,), (1,)), ((), ())),
                preferred_element_type=f32,
            )
            part = jnp.where(widths > q, part, 0.0)
            bnd[at * ROWS : at * ROWS + ROWS, 0:16] = part[:ROWS]


def make_taps(b, mix, mx, wf, bnd, taps):
    for k in range(K):
        mx[pl.ds(k, C, stride=16), :] = mix[b, k].astype(f32)
    coef = bnd[0:144, 0:16].astype(bf16)

    def channels(i, carry):
        for u in range(8):
            c = i * 8 + u
            rhs = jnp.concatenate(
                [mx[pl.ds(c * 32, 16), :], mx[pl.ds(c * 32 + 16, 16), :]], axis=1
            ).astype(bf16)
            out = jnp.dot(coef, rhs, preferred_element_type=f32)
            wf[pl.ds(c * 288, 144), :] = out[:, :C]
            wf[pl.ds(c * 288 + 144, 144), :] = out[:, C:]
        return carry

    lax.fori_loop(0, 8, channels, 0)

    def place(o, carry):
        for q in range(BMAX):
            i = o * BMAX + q
            for l in range(LW):
                w = wf[pl.ds((q * LW + l) * ROWS + o, C, stride=144), :].astype(bf16)
                taps[i, l * C : (l + 1) * C, 0:C] = w
                taps[i, (l + 1) * C : (l + 2) * C, C : 2 * C] = w
        return carry

    lax.fori_loop(0, ROWS, place, 0)


def prep_pairs(s, gain, a, even, odd):
    for p, n in PARTS:
        e = unit(s[pl.ds(p, n), 0:C].astype(f32), gain)
        o = unit(s[pl.ds(p, n), C : 2 * C].astype(f32), gain)
        a[pl.ds(p, n), C : 2 * C] = e.astype(bf16)
        a[pl.ds(p, n), 2 * C : 3 * C] = o.astype(bf16)
        even[pl.ds(8 + p, n), :] = e
        odd[pl.ds(8 + p, n), :] = o
    odd[7:8, :] = odd[367:368, :]
    even[368:369, :] = even[8:9, :]
    a[:, 0:C] = odd[7 : 7 + PAIRS, :].astype(bf16)
    a[:, 3 * C : 4 * C] = even[9 : 9 + PAIRS, :].astype(bf16)


def conv_row(o, start, first, a, s, taps, car):
    base = start[first + o] - first + HALO
    rows = [jnp.clip(base + q, 0, ROWS + 2 * HALO - 1) for q in range(BMAX)]
    for p, n in PARTS:
        acc = jnp.dot(a[rows[0], pl.ds(p, n), :], taps[o * BMAX], preferred_element_type=f32)
        for q in range(1, BMAX):
            acc += jnp.dot(
                a[rows[q], pl.ds(p, n), :], taps[o * BMAX + q], preferred_element_type=f32
            )
        car[pl.ds(p, n), :] = (s[o, pl.ds(p, n), :].astype(f32) + acc).astype(bf16).astype(f32)


def mlp_row(gain, up, down, car, emit):
    for p, n in PARTS:
        rest = jnp.concatenate([car[pl.ds(p, n), :C], car[pl.ds(p, n), C:]], axis=0)
        h = jnp.dot(unit(rest, gain).astype(bf16), up, preferred_element_type=f32)
        h = (0.5 * h * (1.0 + lax.erf(h * 0.7071067811865476))).astype(bf16)
        y = rest + jnp.dot(h, down, preferred_element_type=f32)
        emit(p, n, y[:n], y[n:])


def both(first, second):
    lane = jax.lax.broadcasted_iota(jnp.int32, first.shape, 1)
    return jnp.where(lane < 64, first, pltpu.roll(second, 64, 1))


def step_kernel(
    start, width, x, target, mix, basis, gains, up, down, readout,
    out, score,
    xv, ov, a, s, taps, nrms, fins, mx, wf, cars, cf, bnd, evens, odds,
    halo0, halo1, surf, tgt, snd, rcv,
    x_sem, out_sem, send_sem, recv_sem, ens_send, ens_recv,
):
    me = lax.axis_index("space")
    ens = lax.axis_index("ens")
    members = rcv.shape[0]
    last = lax.axis_size("space") - 1
    barrier = pltpu.get_barrier_semaphore()
    for step in range(1, members):
        pl.semaphore_signal(
            barrier, inc=1, device_id={"ens": lax.rem(ens + step, members)}, device_id_type=MESH
        )

    @pl.when(me > 0)
    def _():
        pl.semaphore_signal(barrier, inc=1, device_id={"space": me - 1}, device_id_type=MESH)

    @pl.when(me < last)
    def _():
        pl.semaphore_signal(barrier, inc=1, device_id={"space": me + 1}, device_id_type=MESH)

    x_copy = pltpu.make_async_copy(x.at[0], xv, x_sem)
    x_copy.start()
    mx[...] = jnp.zeros_like(mx)
    cf[...] = jnp.zeros_like(cf)

    def clear(i, carry):
        taps[i, 3 * C : 4 * C, 0:C] = jnp.zeros((C, C), bf16)
        taps[i, 0:C, C : 2 * C] = jnp.zeros((C, C), bf16)
        return carry

    lax.fori_loop(0, ROWS * BMAX, clear, 0)
    for i in range(HALO):
        a[i] = jnp.zeros((PAIRS, 4 * C), bf16)
        a[ROWS + HALO + i] = jnp.zeros((PAIRS, 4 * C), bf16)
    band_rows(0, me, basis, width, cf, bnd)
    make_taps(0, mix, mx, wf, bnd, taps)

    middle = (me > 0) & (me < last)

    @pl.when(middle)
    def _():
        pl.semaphore_wait(barrier, members + 1)

    @pl.when(jnp.logical_not(middle))
    def _():
        pl.semaphore_wait(barrier, members)

    def forward(b):
        source, landing = (x.at[0], halo0) if b == 0 else (s, halo1)
        return pltpu.make_async_remote_copy(
            src_ref=source.at[pl.ds(ROWS - HALO, HALO)],
            dst_ref=landing.at[pl.ds(0, HALO)],
            send_sem=send_sem.at[b, 0],
            recv_sem=recv_sem.at[b, 0],
            device_id={"space": me + 1},
            device_id_type=MESH,
        )

    def backward(b):
        source, landing = (x.at[0], halo0) if b == 0 else (s, halo1)
        return pltpu.make_async_remote_copy(
            src_ref=source.at[pl.ds(0, HALO)],
            dst_ref=landing.at[pl.ds(HALO, HALO)],
            send_sem=send_sem.at[b, 1],
            recv_sem=recv_sem.at[b, 1],
            device_id={"space": me - 1},
            device_id_type=MESH,
        )

    def send_forward(b):
        @pl.when(me < last)
        def _():
            forward(b).start()

    def send_backward(b):
        @pl.when(me > 0)
        def _():
            backward(b).start()

    send_forward(0)
    send_backward(0)
    first = me * ROWS

    def halo_rows(b, side):
        def fill():
            for i in range(HALO):
                at = side * HALO + i
                row = a.at[side * (ROWS + HALO) + i]
                if b == 0:
                    prep_row(halo0.at[at], gains[0, 0:1], row, None, nrms[i], None)
                else:
                    prep_pairs(halo1.at[at], gains[1, 0:1], row, evens[i], odds[i])

        def empty():
            for i in range(HALO):
                a[side * (ROWS + HALO) + i] = jnp.zeros((PAIRS, 4 * C), bf16)

        has = me > 0 if side == 0 else me < last

        @pl.when(has)
        def _():
            (forward(b) if side == 0 else backward(b)).wait_recv()
            fill()

        @pl.when(jnp.logical_not(has))
        def _():
            empty()

    lead = jnp.concatenate([readout[...].astype(f32), jnp.zeros((14, C), f32)], axis=0).astype(bf16)

    def rows(b, group):
        gain2 = gains[b, 1:2]
        up_matrix, down_matrix = up[b], down[b]
        for o, car in zip(group, cars):
            conv_row(o, start, first, a, s, taps, car)
        for i, (o, car) in enumerate(zip(group, cars)):
            fin = fins[i % 2]

            def emit(p, n, e, d):
                if b == 0:
                    s[o, pl.ds(p, n), 0:C] = e.astype(bf16)
                    s[o, pl.ds(p, n), C : 2 * C] = d.astype(bf16)
                else:
                    fin[pl.ds(2 * p, n, stride=2), :] = e
                    fin[pl.ds(2 * p + 1, n, stride=2), :] = d

            mlp_row(gain2, up_matrix, down_matrix, car, emit)
            if b == 1:
                state = fin[0:LON, :].astype(bf16)
                ov[o] = state
                pltpu.make_async_copy(ov.at[o], out.at[0, o], out_sem.at[o]).start()
                seen = lax.dot_general(
                    lead, state, (((1,), (1,)), ((), ())), preferred_element_type=f32
                )
                surf[pl.ds(o, 1), 0:LON] = seen[0:1]
                surf[pl.ds(16 + o, 1), 0:LON] = seen[1:2]

    def inner_rows(b):
        def some(i, carry):
            rows(b, [HALO + 4 * i + k for k in range(4)])
            return carry

        lax.fori_loop(0, 2, some, 0)

    def outer_rows(b):
        halo_rows(b, 0)
        halo_rows(b, 1)
        rows(b, [0, 1, ROWS - 2, ROWS - 1])

    x_copy.wait()

    def prep0(i, carry):
        for k in range(2):
            o = 2 * i + k
            prep_row(xv.at[o], gains[0, 0:1], a.at[o + HALO], s.at[o], nrms[k], fins[k])
        return carry

    lax.fori_loop(0, ROWS // 2, prep0, 0)
    inner_rows(0)
    outer_rows(0)
    send_backward(1)
    send_forward(1)

    band_rows(1, me, basis, width, cf, bnd)
    make_taps(1, mix, mx, wf, bnd, taps)

    def prep1(i, carry):
        for k in range(2):
            o = 2 * i + k
            prep_pairs(s.at[o], gains[1, 0:1], a.at[o + HALO], evens[k], odds[k])
        return carry

    lax.fori_loop(0, ROWS // 2, prep1, 0)
    inner_rows(1)
    outer_rows(1)

    cols = target.shape[2]
    for e in range(members):
        base = e * cols // 128 * 128
        turn = (256 - (e * cols - base)) % 256
        top = pltpu.roll(surf[0:16, base : base + 256], turn, 1)[:, 0:128]
        low = pltpu.roll(surf[16:32, base : base + 256], turn, 1)[:, 0:128]
        snd[e] = both(top, low).astype(bf16)
    rcv[ens] = snd[ens]

    def deal(step):
        peer = lax.rem(ens + step, members)
        return pltpu.make_async_remote_copy(
            src_ref=snd.at[peer],
            dst_ref=rcv.at[ens],
            send_sem=ens_send.at[step],
            recv_sem=ens_recv.at[ens],
            device_id={"ens": peer},
            device_id_type=MESH,
        )

    for step in range(1, members):
        deal(step).start()
    for o in range(ROWS):
        v = target[o]
        tgt[0, o : o + 1, 0:cols] = v[0:1]
        tgt[1, o : o + 1, 0:cols] = v[1:2]
    for step in range(1, members):
        peer = lax.rem(ens + step, members)
        pltpu.make_async_remote_copy(
            src_ref=snd.at[peer],
            dst_ref=rcv.at[peer],
            send_sem=ens_send.at[step],
            recv_sem=ens_recv.at[peer],
            device_id={"ens": peer},
            device_id_type=MESH,
        ).wait_recv()
    aim = both(tgt[0], tgt[1])
    field = [rcv[m].astype(f32) for m in range(members)]
    skill = sum(jnp.abs(f - aim) for f in field) * (1.0 / members)
    spread = jnp.zeros_like(aim)
    for m in range(members):
        for n in range(m):
            spread = spread + jnp.abs(field[m] - field[n])
    fair = skill - spread * (1.0 / (members * (members - 1)))
    other = pltpu.roll(fair, 64, 1)
    for o in range(ROWS):
        score[o, 0:1, :] = fair[o : o + 1, 0:cols]
        score[o, 1:2, :] = other[o : o + 1, 0:cols]

    for step in range(1, members):
        deal(step).wait_send()
    for b in range(BLOCKS):

        @pl.when(me < last)
        def _():
            forward(b).wait_send()

        @pl.when(me > 0)
        def _():
            backward(b).wait_send()

    def finish(o, carry):
        pltpu.make_async_copy(ov.at[o], out.at[0, o], out_sem.at[o]).wait()
        return carry

    lax.fori_loop(0, ROWS, finish, 0)


def body(
    hidden_vectors, target, mix_weight, basis_coef, rescaling_factors,
    up_weight, down_weight, readout_matrix, band_start, band_width,
):
    members = lax.axis_size("ens")
    vmem = pl.BlockSpec(memory_space=pltpu.VMEM)
    smem = pl.BlockSpec(memory_space=pltpu.SMEM)
    target = target.transpose(1, 0, 2)
    basis_coef = basis_coef.transpose(0, 1, 3, 2, 4)
    state, score = pl.pallas_call(
        step_kernel,
        out_shape=(
            jax.ShapeDtypeStruct(hidden_vectors.shape, bf16),
            jax.ShapeDtypeStruct(target.shape, f32),
        ),
        in_specs=[smem, smem, pl.BlockSpec(memory_space=pl.ANY)] + [vmem] * 7,
        out_specs=(pl.BlockSpec(memory_space=pl.ANY), vmem),
        scratch_shapes=[
            pltpu.VMEM((ROWS, LON, C), bf16),
            pltpu.VMEM((ROWS, LON, C), bf16),
            pltpu.VMEM((ROWS + 2 * HALO, PAIRS, 4 * C), bf16),
            pltpu.VMEM((ROWS, PAIRS, 2 * C), bf16),
            pltpu.VMEM((ROWS * BMAX, 4 * C, 2 * C), bf16),
            [pltpu.VMEM((752, C), f32)] * 2,
            [pltpu.VMEM((2 * PAIRS, C), f32)] * 2,
            pltpu.VMEM((16 * C, C), f32),
            pltpu.VMEM((144 * C, C), f32),
            [pltpu.VMEM((PAIRS, 2 * C), f32)] * 4,
            pltpu.VMEM((192, 256), f32),
            pltpu.VMEM((144, C), f32),
            [pltpu.VMEM((384, C), f32)] * 2,
            [pltpu.VMEM((384, C), f32)] * 2,
            pltpu.VMEM((2 * HALO, LON, C), bf16),
            pltpu.VMEM((2 * HALO, PAIRS, 2 * C), bf16),
            pltpu.VMEM((32, 896), f32),
            pltpu.VMEM((2, 16, 128), f32),
            pltpu.VMEM((members, 16, 128), bf16),
            pltpu.VMEM((members, 16, 128), bf16),
            pltpu.SemaphoreType.DMA,
            pltpu.SemaphoreType.DMA((ROWS,)),
            pltpu.SemaphoreType.DMA((2, 2)),
            pltpu.SemaphoreType.DMA((2, 2)),
            pltpu.SemaphoreType.DMA((members,)),
            pltpu.SemaphoreType.DMA((members,)),
        ],
        compiler_params=pltpu.CompilerParams(
            vmem_limit_bytes=56 * 2**20, collective_id=0, has_side_effects=True
        ),
    )(
        band_start, band_width, hidden_vectors, target, mix_weight, basis_coef,
        rescaling_factors, up_weight, down_weight, readout_matrix,
    )
    return state, score.transpose(1, 0, 2)


def solution(mesh):
    in_specs = (P("ens", "space", None, None), P(None, "space", "ens")) + (P(),) * 8
    out_specs = (P("ens", "space", None, None), P(None, "space", "ens"))
    return jax.shard_map(body, mesh=mesh, in_specs=in_specs, out_specs=out_specs, check_vma=False)
```

```python
import jax
import jax.numpy as jnp
from jax import lax
from jax.experimental import pallas as pl
from jax.experimental.pallas import tpu as pltpu
from jax.sharding import PartitionSpec as P

K = 9
BMAX = 4
HALO = 2
LW = 3
BLOCKS = 2
ROWS = 12
LON = 720
PAIRS = 368
C = 128
STEP = 80
PARTS = ((0, 192), (192, 176))
f32 = jnp.float32
bf16 = jnp.bfloat16
SPAN = 145
MESH = pl.DeviceIdType.MESH


def unit(v, gain):
    return v * lax.rsqrt(jnp.mean(v * v, axis=-1, keepdims=True) + 1e-6) * gain


def prep_row(x, gain, a, s, nrm, raw):
    for t in range(0, LON, STEP):
        v = x[pl.ds(t, STEP), :].astype(f32)
        nrm[pl.ds(8 + t, STEP), :] = unit(v, gain)
        if s is not None:
            raw[pl.ds(t, STEP), :] = v
    nrm[7:8, :] = nrm[727:728, :]
    nrm[728:729, :] = nrm[8:9, :]
    for j in range(4):
        a[:, j * C : (j + 1) * C] = nrm[pl.ds(7 + j, PAIRS, stride=2), :].astype(bf16)
    if s is not None:
        for j in range(2):
            s[:, j * C : (j + 1) * C] = raw[pl.ds(j, PAIRS, stride=2), :].astype(bf16)


def band_rows(b, me, basis, width, cf, bnd):
    lat = jax.lax.broadcasted_iota(jnp.int32, (16, 192), 1)
    own = jax.lax.broadcasted_iota(jnp.int32, (16, 192), 0)
    pick = jnp.where((lat == own + me * ROWS) & (own < ROWS), 1.0, 0.0).astype(bf16)
    row = jax.lax.broadcasted_iota(jnp.int32, (16, 16), 0)
    widths = jnp.zeros((16, 16), jnp.int32)
    for o in range(ROWS):
        widths = jnp.where(row == o, width[me * ROWS + o], widths)
    for k in range(K):
        for l in range(LW):
            v = basis[b, k, l].astype(f32)
            for q in range(BMAX):
                at = (q * LW + l) * 16 + k
                cf[at : at + 1, 0:192] = v[q : q + 1]
    for q in range(BMAX):
        for l in range(LW):
            at = q * LW + l
            part = lax.dot_general(
                pick,
                cf[at * 16 : at * 16 + 16, 0:192].astype(bf16),
                (((1,), (1,)), ((), ())),
                preferred_element_type=f32,
            )
            part = jnp.where(widths > q, part, 0.0)
            bnd[at * ROWS : at * ROWS + ROWS, 0:16] = part[:ROWS]


def spread_mix(b, mix, mx):
    for k in range(K):
        mx[pl.ds(k, C, stride=16), :] = mix[b, k].astype(f32)


def channels(coef, mx, wf, low, count):
    for u in range(count):
        c = low + u
        rhs = jnp.concatenate(
            [mx[pl.ds(c * 32, 16), :], mx[pl.ds(c * 32 + 16, 16), :]], axis=1
        ).astype(bf16)
        out = jnp.dot(coef, rhs, preferred_element_type=f32)
        wf[pl.ds(c * 2 * SPAN, 144), :] = out[:, :C]
        wf[pl.ds(c * 2 * SPAN + SPAN, 144), :] = out[:, C:]


def place(o, wf, taps):
    for q in range(BMAX):
        i = o * BMAX + q
        for l in range(LW):
            w = wf[pl.ds((q * LW + l) * ROWS + o, C, stride=SPAN), :].astype(bf16)
            taps[i, l * C : (l + 1) * C, 0:C] = w
            taps[i, (l + 1) * C : (l + 2) * C, C : 2 * C] = w


def make_taps(bnd, mx, wf, taps):
    coef = bnd[0:144, 0:16].astype(bf16)

    def some(i, carry):
        channels(coef, mx, wf, i * 16, 16)
        return carry

    def put(o, carry):
        place(o, wf, taps)
        return carry

    lax.fori_loop(0, 4, some, 0)
    lax.fori_loop(0, ROWS, put, 0)


def prep_pairs(s, gain, a, even, odd):
    for p, n in PARTS:
        e = unit(s[pl.ds(p, n), 0:C].astype(f32), gain)
        o = unit(s[pl.ds(p, n), C : 2 * C].astype(f32), gain)
        a[pl.ds(p, n), C : 2 * C] = e.astype(bf16)
        a[pl.ds(p, n), 2 * C : 3 * C] = o.astype(bf16)
        even[pl.ds(8 + p, n), :] = e
        odd[pl.ds(8 + p, n), :] = o
    odd[7:8, :] = odd[367:368, :]
    even[368:369, :] = even[8:9, :]
    a[:, 0:C] = odd[7 : 7 + PAIRS, :].astype(bf16)
    a[:, 3 * C : 4 * C] = even[9 : 9 + PAIRS, :].astype(bf16)


def conv_row(o, start, first, a, s, taps, car):
    base = start[first + o] - first + HALO
    rows = [jnp.clip(base + q, 0, ROWS + 2 * HALO - 1) for q in range(BMAX)]
    for p, n in PARTS:
        acc = jnp.dot(a[rows[0], pl.ds(p, n), :], taps[o * BMAX], preferred_element_type=f32)
        for q in range(1, BMAX):
            acc += jnp.dot(
                a[rows[q], pl.ds(p, n), :], taps[o * BMAX + q], preferred_element_type=f32
            )
        car[pl.ds(p, n), :] = (s[o, pl.ds(p, n), :].astype(f32) + acc).astype(bf16).astype(f32)


def mlp_row(gain, up, down, car, emit):
    for p, n in PARTS:
        rest = jnp.concatenate([car[pl.ds(p, n), :C], car[pl.ds(p, n), C:]], axis=0)
        h = jnp.dot(unit(rest, gain).astype(bf16), up, preferred_element_type=f32)
        h = (0.5 * h * (1.0 + lax.erf(h * 0.7071067811865476))).astype(bf16)
        y = rest + jnp.dot(h, down, preferred_element_type=f32)
        emit(p, n, y[:n], y[n:])


def both(first, second):
    lane = jax.lax.broadcasted_iota(jnp.int32, first.shape, 1)
    return jnp.where(lane < 64, first, pltpu.roll(second, 64, 1))


def step_kernel(
    start, width, x, mix, basis, gains, up, down, readout,
    out, got,
    xv, a, s, taps_by_block, nrms, fins, mx, wf, cars, cf, bnd, evens, odds,
    halo0, halo1, surf, snd, rcv, leads, seen,
    x_sem, out_sem, send_sem, recv_sem, ens_send, ens_recv,
):
    me = lax.axis_index("space")
    ens = lax.axis_index("ens")
    members = rcv.shape[0]
    last = lax.axis_size("space") - 1
    barrier = pltpu.get_barrier_semaphore()
    for step in range(1, members):
        pl.semaphore_signal(
            barrier, inc=1, device_id={"ens": lax.rem(ens + step, members)}, device_id_type=MESH
        )

    @pl.when(me > 0)
    def _():
        pl.semaphore_signal(barrier, inc=1, device_id={"space": me - 1}, device_id_type=MESH)

    @pl.when(me < last)
    def _():
        pl.semaphore_signal(barrier, inc=1, device_id={"space": me + 1}, device_id_type=MESH)

    x_copy = pltpu.make_async_copy(x.at[0], xv, x_sem)
    x_copy.start()
    mx[...] = jnp.zeros_like(mx)
    cf[...] = jnp.zeros_like(cf)

    def clear(i, carry):
        for taps in taps_by_block:
            taps[i, 3 * C : 4 * C, 0:C] = jnp.zeros((C, C), bf16)
            taps[i, 0:C, C : 2 * C] = jnp.zeros((C, C), bf16)
        return carry

    lax.fori_loop(0, ROWS * BMAX, clear, 0)
    for i in range(HALO):
        a[i] = jnp.zeros((PAIRS, 4 * C), bf16)
        a[ROWS + HALO + i] = jnp.zeros((PAIRS, 4 * C), bf16)
    band_rows(0, me, basis, width, cf, bnd)
    spread_mix(0, mix, mx)
    make_taps(bnd, mx, wf, taps_by_block[0])
    band_rows(1, me, basis, width, cf, bnd)
    spread_mix(1, mix, mx)

    middle = (me > 0) & (me < last)

    @pl.when(middle)
    def _():
        pl.semaphore_wait(barrier, members + 1)

    @pl.when(jnp.logical_not(middle))
    def _():
        pl.semaphore_wait(barrier, members)

    def forward(b):
        source, landing = (x.at[0], halo0) if b == 0 else (s, halo1)
        return pltpu.make_async_remote_copy(
            src_ref=source.at[pl.ds(ROWS - HALO, HALO)],
            dst_ref=landing.at[pl.ds(0, HALO)],
            send_sem=send_sem.at[b, 0],
            recv_sem=recv_sem.at[b, 0],
            device_id={"space": me + 1},
            device_id_type=MESH,
        )

    def backward(b):
        source, landing = (x.at[0], halo0) if b == 0 else (s, halo1)
        return pltpu.make_async_remote_copy(
            src_ref=source.at[pl.ds(0, HALO)],
            dst_ref=landing.at[pl.ds(HALO, HALO)],
            send_sem=send_sem.at[b, 1],
            recv_sem=recv_sem.at[b, 1],
            device_id={"space": me - 1},
            device_id_type=MESH,
        )

    def send_forward(b):
        @pl.when(me < last)
        def _():
            forward(b).start()

    def send_backward(b):
        @pl.when(me > 0)
        def _():
            backward(b).start()

    send_forward(0)
    send_backward(0)
    first = me * ROWS

    def halo_rows(b, side):
        def fill():
            for i in range(HALO):
                at = side * HALO + i
                row = a.at[side * (ROWS + HALO) + i]
                if b == 0:
                    prep_row(halo0.at[at], gains[0, 0:1], row, None, nrms[i], None)
                else:
                    prep_pairs(halo1.at[at], gains[1, 0:1], row, evens[i], odds[i])

        def empty():
            for i in range(HALO):
                a[side * (ROWS + HALO) + i] = jnp.zeros((PAIRS, 4 * C), bf16)

        has = me > 0 if side == 0 else me < last

        @pl.when(has)
        def _():
            (forward(b) if side == 0 else backward(b)).wait_recv()
            fill()

        @pl.when(jnp.logical_not(has))
        def _():
            empty()

    turned = jnp.concatenate([readout[...].astype(f32), jnp.zeros((C - 2, C), f32)], axis=0).T
    seen_lane = jax.lax.broadcasted_iota(jnp.int32, (C, C), 1)
    for o in range(ROWS):
        for side in range(2):
            at = 32 * side + o
            lead = jnp.where(seen_lane == at, turned[:, 0:1], 0.0)
            lead = jnp.where(seen_lane == at + 16, turned[:, 1:2], lead)
            leads[o, side * C : (side + 1) * C, :] = lead.astype(bf16)
    seen[...] = jnp.zeros_like(seen)

    def rows(b, group):
        taps = taps_by_block[b]
        gain2 = gains[b, 1:2]
        up_matrix, down_matrix = up[b], down[b]
        for o, car in zip(group, cars):
            conv_row(o, start, first, a, s, taps, car)
        for i, (o, car) in enumerate(zip(group, cars)):
            fin = fins[i % 2]

            def emit(p, n, e, d):
                if b == 0:
                    s[o, pl.ds(p, n), 0:C] = e.astype(bf16)
                    s[o, pl.ds(p, n), C : 2 * C] = d.astype(bf16)
                else:
                    fin[pl.ds(2 * p, n, stride=2), :] = e
                    fin[pl.ds(2 * p + 1, n, stride=2), :] = d
                    pair = jnp.concatenate([e.astype(bf16), d.astype(bf16)], axis=1)
                    seen[pl.ds(p, n), :] += jnp.dot(
                        pair, leads[o], preferred_element_type=f32
                    )

            mlp_row(gain2, up_matrix, down_matrix, car, emit)
            if b == 1:
                xv[o] = fin[0:LON, :].astype(bf16)
                pltpu.make_async_copy(xv.at[o], out.at[0, o], out_sem.at[o]).start()

    def inner_rows(b):
        def some(i, carry):
            rows(b, [HALO + 4 * i + k for k in range(4)])
            if b == 0:
                channels(bnd[0:144, 0:16].astype(bf16), mx, wf, i * 32, 32)
            return carry

        lax.fori_loop(0, 2, some, 0)

    def outer_rows(b):
        halo_rows(b, 0)
        halo_rows(b, 1)
        rows(b, [0, 1, ROWS - 2, ROWS - 1])
        if b == 0:
            for o in range(ROWS):
                place(o, wf, taps_by_block[1])

    x_copy.wait()

    def prep0(i, carry):
        for k in range(2):
            o = 2 * i + k
            prep_row(xv.at[o], gains[0, 0:1], a.at[o + HALO], s.at[o], nrms[k], fins[k])
        return carry

    lax.fori_loop(0, ROWS // 2, prep0, 0)
    inner_rows(0)
    outer_rows(0)
    send_backward(1)
    send_forward(1)


    def prep1(i, carry):
        for k in range(2):
            o = 2 * i + k
            prep_pairs(s.at[o], gains[1, 0:1], a.at[o + HALO], evens[k], odds[k])
        return carry

    lax.fori_loop(0, ROWS // 2, prep1, 0)
    inner_rows(1)
    outer_rows(1)

    fin = fins[0]
    fin[pl.ds(0, PAIRS, stride=2), :] = seen[...]
    fin[pl.ds(1, PAIRS, stride=2), :] = pltpu.roll(seen[...], C - 32, 1)
    for t in range(0, 640, C):
        surf[:, t : t + C] = fin[t : t + C, :].T[0:32]
    surf[:, 640:736] = fin[640:736, :].T[0:32]
    cols = LON // members
    for e in range(members):
        base = e * cols // 128 * 128
        turn = (256 - (e * cols - base)) % 256
        top = pltpu.roll(surf[0:16, base : base + 256], turn, 1)[:, 0:128]
        low = pltpu.roll(surf[16:32, base : base + 256], turn, 1)[:, 0:128]
        snd[e] = both(top, low).astype(bf16)
    rcv[ens] = snd[ens]

    def deal(step):
        peer = lax.rem(ens + step, members)
        return pltpu.make_async_remote_copy(
            src_ref=snd.at[peer],
            dst_ref=rcv.at[ens],
            send_sem=ens_send.at[step],
            recv_sem=ens_recv.at[ens],
            device_id={"ens": peer},
            device_id_type=MESH,
        )

    for step in range(1, members):
        deal(step).start()
    for step in range(1, members):
        peer = lax.rem(ens + step, members)
        pltpu.make_async_remote_copy(
            src_ref=snd.at[peer],
            dst_ref=rcv.at[peer],
            send_sem=ens_send.at[step],
            recv_sem=ens_recv.at[peer],
            device_id={"ens": peer},
            device_id_type=MESH,
        ).wait_recv()
    got[...] = rcv[...]
    for step in range(1, members):
        deal(step).wait_send()
    for b in range(BLOCKS):

        @pl.when(me < last)
        def _():
            forward(b).wait_send()

        @pl.when(me > 0)
        def _():
            backward(b).wait_send()

    def finish(o, carry):
        pltpu.make_async_copy(xv.at[o], out.at[0, o], out_sem.at[o]).wait()
        return carry

    lax.fori_loop(0, ROWS, finish, 0)


def score_kernel(
    state, got_far, target_far, out, score_far, held, got, target, score, tgt, in_sems, sems, small
):
    ins = [
        pltpu.make_async_copy(got_far, got, small.at[0]),
        pltpu.make_async_copy(target_far, target, small.at[1]),
    ]
    for copy in ins:
        copy.start()
    arrivals = [
        pltpu.make_async_copy(state.at[0, o], held.at[o], in_sems.at[o]) for o in range(ROWS)
    ]
    copies = [pltpu.make_async_copy(held.at[o], out.at[0, o], sems.at[o]) for o in range(ROWS)]
    for arrival in arrivals:
        arrival.start()
    for arrival, copy in zip(arrivals, copies):
        arrival.wait()
        copy.start()
    for copy in ins:
        copy.wait()
    members, cols = got.shape[0], target.shape[2]
    for o in range(ROWS):
        v = target[o]
        tgt[0, o : o + 1, 0:cols] = v[0:1]
        tgt[1, o : o + 1, 0:cols] = v[1:2]
    aim = both(tgt[0], tgt[1])
    field = [got[m].astype(f32) for m in range(members)]
    skill = sum(jnp.abs(f - aim) for f in field) * (1.0 / members)
    spread = jnp.zeros_like(aim)
    for m in range(members):
        for n in range(m):
            spread = spread + jnp.abs(field[m] - field[n])
    fair = skill - spread * (1.0 / (members * (members - 1)))
    other = pltpu.roll(fair, 64, 1)
    for o in range(ROWS):
        score[o, 0:1, :] = fair[o : o + 1, 0:cols]
        score[o, 1:2, :] = other[o : o + 1, 0:cols]
    result = pltpu.make_async_copy(score, score_far, small.at[2])
    result.start()
    result.wait()
    for copy in copies:
        copy.wait()


def body(
    hidden_vectors, target, mix_weight, basis_coef, rescaling_factors,
    up_weight, down_weight, readout_matrix, band_start, band_width,
):
    members = lax.axis_size("ens")
    vmem = pl.BlockSpec(memory_space=pltpu.VMEM)
    smem = pl.BlockSpec(memory_space=pltpu.SMEM)
    basis_coef = basis_coef.transpose(0, 1, 3, 2, 4)
    state, surfaces = pl.pallas_call(
        step_kernel,
        out_shape=(
            jax.ShapeDtypeStruct(hidden_vectors.shape, bf16),
            jax.ShapeDtypeStruct((members, 16, 128), bf16),
        ),
        in_specs=[smem, smem, pl.BlockSpec(memory_space=pl.ANY)] + [vmem] * 6,
        out_specs=(pl.BlockSpec(memory_space=pl.ANY), vmem),
        scratch_shapes=[
            pltpu.VMEM((ROWS, LON, C), bf16),
            pltpu.VMEM((ROWS + 2 * HALO, PAIRS, 4 * C), bf16),
            pltpu.VMEM((ROWS, PAIRS, 2 * C), bf16),
            [pltpu.VMEM((ROWS * BMAX, 4 * C, 2 * C), bf16)] * 2,
            [pltpu.VMEM((752, C), f32)] * 2,
            [pltpu.VMEM((2 * PAIRS, C), f32)] * 2,
            pltpu.VMEM((16 * C, C), f32),
            pltpu.VMEM((SPAN * C, C), f32),
            [pltpu.VMEM((PAIRS, 2 * C), f32)] * 4,
            pltpu.VMEM((192, 256), f32),
            pltpu.VMEM((144, C), f32),
            [pltpu.VMEM((384, C), f32)] * 2,
            [pltpu.VMEM((384, C), f32)] * 2,
            pltpu.VMEM((2 * HALO, LON, C), bf16),
            pltpu.VMEM((2 * HALO, PAIRS, 2 * C), bf16),
            pltpu.VMEM((32, 896), f32),
            pltpu.VMEM((members, 16, 128), bf16),
            pltpu.VMEM((members, 16, 128), bf16),
            pltpu.VMEM((ROWS, 2 * C, C), bf16),
            pltpu.VMEM((PAIRS, C), f32),
            pltpu.SemaphoreType.DMA,
            pltpu.SemaphoreType.DMA((ROWS,)),
            pltpu.SemaphoreType.DMA((2, 2)),
            pltpu.SemaphoreType.DMA((2, 2)),
            pltpu.SemaphoreType.DMA((members,)),
            pltpu.SemaphoreType.DMA((members,)),
        ],
        compiler_params=pltpu.CompilerParams(
            vmem_limit_bytes=60 * 2**20, collective_id=0, has_side_effects=True
        ),
    )(
        band_start, band_width, hidden_vectors, mix_weight, basis_coef,
        rescaling_factors, up_weight, down_weight, readout_matrix,
    )
    target = target.transpose(1, 0, 2)
    state, score = pl.pallas_call(
        score_kernel,
        out_shape=(
            jax.ShapeDtypeStruct(state.shape, bf16),
            jax.ShapeDtypeStruct(target.shape, f32),
        ),
        in_specs=[pl.BlockSpec(memory_space=pl.ANY)] * 3,
        out_specs=[pl.BlockSpec(memory_space=pl.ANY)] * 2,
        scratch_shapes=[
            pltpu.VMEM((ROWS, LON, C), bf16),
            pltpu.VMEM(surfaces.shape, bf16),
            pltpu.VMEM(target.shape, f32),
            pltpu.VMEM(target.shape, f32),
            pltpu.VMEM((2, 16, 128), f32),
            pltpu.SemaphoreType.DMA((ROWS,)),
            pltpu.SemaphoreType.DMA((ROWS,)),
            pltpu.SemaphoreType.DMA((3,)),
        ],
    )(state, surfaces, target)
    return state, score.transpose(1, 0, 2)


def solution(mesh):
    in_specs = (P("ens", "space", None, None), P(None, "space", "ens")) + (P(),) * 8
    out_specs = (P("ens", "space", None, None), P(None, "space", "ens"))
    return jax.shard_map(body, mesh=mesh, in_specs=in_specs, out_specs=out_specs, check_vma=False)
```

```python
import jax
import jax.numpy as jnp
from jax import lax
from jax.experimental import pallas as pl
from jax.experimental.pallas import tpu as pltpu
from jax.sharding import PartitionSpec as P

K = 9
BMAX = 4
HALO = 2
LW = 3
BLOCKS = 2
ROWS = 12
LON = 720
PAIRS = 368
C = 128
STEP = 80
PARTS = ((0, 192), (192, 176))
f32 = jnp.float32
bf16 = jnp.bfloat16
SPAN = 145
MESH = pl.DeviceIdType.MESH


def unit(v, gain):
    return v * lax.rsqrt(jnp.mean(v * v, axis=-1, keepdims=True) + 1e-6) * gain


def prep_row(x, gain, a, s, nrm, raw):
    for t in range(0, LON, STEP):
        v = x[pl.ds(t, STEP), :].astype(f32)
        nrm[pl.ds(8 + t, STEP), :] = unit(v, gain)
        if s is not None:
            raw[pl.ds(t, STEP), :] = v
    nrm[7:8, :] = nrm[727:728, :]
    nrm[728:729, :] = nrm[8:9, :]
    for j in range(4):
        a[:, j * C : (j + 1) * C] = nrm[pl.ds(7 + j, PAIRS, stride=2), :].astype(bf16)
    if s is not None:
        for j in range(2):
            s[:, j * C : (j + 1) * C] = raw[pl.ds(j, PAIRS, stride=2), :].astype(bf16)


def band_rows(b, me, basis, width, cf, bnd):
    lat = jax.lax.broadcasted_iota(jnp.int32, (16, 192), 1)
    own = jax.lax.broadcasted_iota(jnp.int32, (16, 192), 0)
    pick = jnp.where((lat == own + me * ROWS) & (own < ROWS), 1.0, 0.0).astype(bf16)
    row = jax.lax.broadcasted_iota(jnp.int32, (16, 16), 0)
    widths = jnp.zeros((16, 16), jnp.int32)
    for o in range(ROWS):
        widths = jnp.where(row == o, width[me * ROWS + o], widths)
    for k in range(K):
        for l in range(LW):
            v = basis[b, k, l].astype(f32)
            for q in range(BMAX):
                at = (q * LW + l) * 16 + k
                cf[at : at + 1, 0:192] = v[q : q + 1]
    for q in range(BMAX):
        for l in range(LW):
            at = q * LW + l
            part = lax.dot_general(
                pick,
                cf[at * 16 : at * 16 + 16, 0:192].astype(bf16),
                (((1,), (1,)), ((), ())),
                preferred_element_type=f32,
            )
            part = jnp.where(widths > q, part, 0.0)
            bnd[at * ROWS : at * ROWS + ROWS, 0:16] = part[:ROWS]


def spread_mix(b, mix, mx):
    for k in range(K):
        mx[pl.ds(k, C, stride=16), :] = mix[b, k].astype(f32)


def channels(coef, mx, wf, low, count):
    for u in range(count):
        c = low + u
        rhs = jnp.concatenate(
            [mx[pl.ds(c * 32, 16), :], mx[pl.ds(c * 32 + 16, 16), :]], axis=1
        ).astype(bf16)
        out = jnp.dot(coef, rhs, preferred_element_type=f32)
        wf[pl.ds(c * 2 * SPAN, 144), :] = out[:, :C]
        wf[pl.ds(c * 2 * SPAN + SPAN, 144), :] = out[:, C:]


def place(o, wf, taps):
    for q in range(BMAX):
        i = o * BMAX + q
        for l in range(LW):
            w = wf[pl.ds((q * LW + l) * ROWS + o, C, stride=SPAN), :].astype(bf16)
            taps[i, l * C : (l + 1) * C, 0:C] = w
            taps[i, (l + 1) * C : (l + 2) * C, C : 2 * C] = w


def taps_beside(prepare, bnd, mx, wf, taps):
    coef = bnd[0:144, 0:16].astype(bf16)

    def some(i, carry):
        for k in range(3):
            prepare(3 * i + k, k)
        channels(coef, mx, wf, i * 16, 16)
        return carry

    def put(o, carry):
        place(o, wf, taps)
        return carry

    lax.fori_loop(0, 4, some, 0)
    lax.fori_loop(0, ROWS, put, 0)


def prep_pairs(s, gain, a, even, odd):
    for p, n in PARTS:
        e = unit(s[pl.ds(p, n), 0:C].astype(f32), gain)
        o = unit(s[pl.ds(p, n), C : 2 * C].astype(f32), gain)
        a[pl.ds(p, n), C : 2 * C] = e.astype(bf16)
        a[pl.ds(p, n), 2 * C : 3 * C] = o.astype(bf16)
        even[pl.ds(8 + p, n), :] = e
        odd[pl.ds(8 + p, n), :] = o
    odd[7:8, :] = odd[367:368, :]
    even[368:369, :] = even[8:9, :]
    a[:, 0:C] = odd[7 : 7 + PAIRS, :].astype(bf16)
    a[:, 3 * C : 4 * C] = even[9 : 9 + PAIRS, :].astype(bf16)


def conv_row(o, start, first, a, s, taps, car):
    base = start[first + o] - first + HALO
    rows = [jnp.clip(base + q, 0, ROWS + 2 * HALO - 1) for q in range(BMAX)]
    for p, n in PARTS:
        acc = jnp.dot(a[rows[0], pl.ds(p, n), :], taps[o * BMAX], preferred_element_type=f32)
        for q in range(1, BMAX):
            acc += jnp.dot(
                a[rows[q], pl.ds(p, n), :], taps[o * BMAX + q], preferred_element_type=f32
            )
        car[pl.ds(p, n), :] = (s[o, pl.ds(p, n), :].astype(f32) + acc).astype(bf16).astype(f32)


def mlp_row(gain, up, down, car, emit):
    for p, n in PARTS:
        rest = jnp.concatenate([car[pl.ds(p, n), :C], car[pl.ds(p, n), C:]], axis=0)
        h = jnp.dot(unit(rest, gain).astype(bf16), up, preferred_element_type=f32)
        h = (0.5 * h * (1.0 + lax.erf(h * 0.7071067811865476))).astype(bf16)
        y = rest + jnp.dot(h, down, preferred_element_type=f32)
        emit(p, n, y[:n], y[n:])


def both(first, second):
    lane = jax.lax.broadcasted_iota(jnp.int32, first.shape, 1)
    return jnp.where(lane < 64, first, pltpu.roll(second, 64, 1))


def step_kernel(
    start, width, x, mix, basis, gains, up, down, readout,
    out, got,
    xv, a, s, taps, nrms, fins, mx, wf, cars, cf, bnd, evens, odds,
    halo0, halo1, surf, snd, rcv, leads, seen,
    x_sem, out_sem, send_sem, recv_sem, ens_send, ens_recv,
):
    me = lax.axis_index("space")
    ens = lax.axis_index("ens")
    members = rcv.shape[0]
    last = lax.axis_size("space") - 1
    barrier = pltpu.get_barrier_semaphore()
    for step in range(1, members):
        pl.semaphore_signal(
            barrier, inc=1, device_id={"ens": lax.rem(ens + step, members)}, device_id_type=MESH
        )

    @pl.when(me > 0)
    def _():
        pl.semaphore_signal(barrier, inc=1, device_id={"space": me - 1}, device_id_type=MESH)

    @pl.when(me < last)
    def _():
        pl.semaphore_signal(barrier, inc=1, device_id={"space": me + 1}, device_id_type=MESH)

    x_copy = pltpu.make_async_copy(x.at[0], xv, x_sem)
    x_copy.start()
    mx[...] = jnp.zeros_like(mx)
    cf[...] = jnp.zeros_like(cf)

    def clear(i, carry):
        taps[i, 3 * C : 4 * C, 0:C] = jnp.zeros((C, C), bf16)
        taps[i, 0:C, C : 2 * C] = jnp.zeros((C, C), bf16)
        return carry

    lax.fori_loop(0, ROWS * BMAX, clear, 0)
    for i in range(HALO):
        a[i] = jnp.zeros((PAIRS, 4 * C), bf16)
        a[ROWS + HALO + i] = jnp.zeros((PAIRS, 4 * C), bf16)
    band_rows(0, me, basis, width, cf, bnd)
    spread_mix(0, mix, mx)

    middle = (me > 0) & (me < last)

    @pl.when(middle)
    def _():
        pl.semaphore_wait(barrier, members + 1)

    @pl.when(jnp.logical_not(middle))
    def _():
        pl.semaphore_wait(barrier, members)

    def forward(b):
        source, landing = (x.at[0], halo0) if b == 0 else (s, halo1)
        return pltpu.make_async_remote_copy(
            src_ref=source.at[pl.ds(ROWS - HALO, HALO)],
            dst_ref=landing.at[pl.ds(0, HALO)],
            send_sem=send_sem.at[b, 0],
            recv_sem=recv_sem.at[b, 0],
            device_id={"space": me + 1},
            device_id_type=MESH,
        )

    def backward(b):
        source, landing = (x.at[0], halo0) if b == 0 else (s, halo1)
        return pltpu.make_async_remote_copy(
            src_ref=source.at[pl.ds(0, HALO)],
            dst_ref=landing.at[pl.ds(HALO, HALO)],
            send_sem=send_sem.at[b, 1],
            recv_sem=recv_sem.at[b, 1],
            device_id={"space": me - 1},
            device_id_type=MESH,
        )

    def send_forward(b):
        @pl.when(me < last)
        def _():
            forward(b).start()

    def send_backward(b):
        @pl.when(me > 0)
        def _():
            backward(b).start()

    send_forward(0)
    send_backward(0)
    first = me * ROWS

    def halo_rows(b, side):
        def fill():
            for i in range(HALO):
                at = side * HALO + i
                row = a.at[side * (ROWS + HALO) + i]
                if b == 0:
                    prep_row(halo0.at[at], gains[0, 0:1], row, None, nrms[i], None)
                else:
                    prep_pairs(halo1.at[at], gains[1, 0:1], row, evens[i], odds[i])

        def empty():
            for i in range(HALO):
                a[side * (ROWS + HALO) + i] = jnp.zeros((PAIRS, 4 * C), bf16)

        has = me > 0 if side == 0 else me < last

        @pl.when(has)
        def _():
            (forward(b) if side == 0 else backward(b)).wait_recv()
            fill()

        @pl.when(jnp.logical_not(has))
        def _():
            empty()

    turned = jnp.concatenate([readout[...].astype(f32), jnp.zeros((C - 2, C), f32)], axis=0).T
    seen_lane = jax.lax.broadcasted_iota(jnp.int32, (C, C), 1)
    for o in range(ROWS):
        for side in range(2):
            at = 32 * side + o
            lead = jnp.where(seen_lane == at, turned[:, 0:1], 0.0)
            lead = jnp.where(seen_lane == at + 16, turned[:, 1:2], lead)
            leads[o, side * C : (side + 1) * C, :] = lead.astype(bf16)
    seen[...] = jnp.zeros_like(seen)

    def rows(b, group):
        gain2 = gains[b, 1:2]
        up_matrix, down_matrix = up[b], down[b]
        for o, car in zip(group, cars):
            conv_row(o, start, first, a, s, taps, car)
        for i, (o, car) in enumerate(zip(group, cars)):
            fin = fins[i % 2]

            def emit(p, n, e, d):
                if b == 0:
                    s[o, pl.ds(p, n), 0:C] = e.astype(bf16)
                    s[o, pl.ds(p, n), C : 2 * C] = d.astype(bf16)
                else:
                    fin[pl.ds(2 * p, n, stride=2), :] = e
                    fin[pl.ds(2 * p + 1, n, stride=2), :] = d
                    pair = jnp.concatenate([e.astype(bf16), d.astype(bf16)], axis=1)
                    seen[pl.ds(p, n), :] += jnp.dot(
                        pair, leads[o], preferred_element_type=f32
                    )

            mlp_row(gain2, up_matrix, down_matrix, car, emit)
            if b == 1:
                xv[o] = fin[0:LON, :].astype(bf16)
                pltpu.make_async_copy(xv.at[o], out.at[0, o], out_sem.at[o]).start()

    def inner_rows(b):
        def some(i, carry):
            rows(b, [HALO + 4 * i + k for k in range(4)])
            return carry

        lax.fori_loop(0, 2, some, 0)

    def outer_rows(b):
        halo_rows(b, 0)
        halo_rows(b, 1)
        rows(b, [0, 1, ROWS - 2, ROWS - 1])

    x_copy.wait()

    def prep0(o, k):
        prep_row(xv.at[o], gains[0, 0:1], a.at[o + HALO], s.at[o], nrms[k], fins[k])

    taps_beside(prep0, bnd, mx, wf, taps)
    inner_rows(0)
    outer_rows(0)
    send_backward(1)
    send_forward(1)

    band_rows(1, me, basis, width, cf, bnd)
    spread_mix(1, mix, mx)

    def prep1(o, k):
        prep_pairs(s.at[o], gains[1, 0:1], a.at[o + HALO], evens[k], odds[k])

    taps_beside(prep1, bnd, mx, wf, taps)
    inner_rows(1)
    outer_rows(1)

    fin = fins[0]
    fin[pl.ds(0, PAIRS, stride=2), :] = seen[...]
    fin[pl.ds(1, PAIRS, stride=2), :] = pltpu.roll(seen[...], C - 32, 1)
    for t in range(0, 640, C):
        surf[:, t : t + C] = fin[t : t + C, :].T[0:32]
    surf[:, 640:736] = fin[640:736, :].T[0:32]
    cols = LON // members
    for e in range(members):
        base = e * cols // 128 * 128
        turn = (256 - (e * cols - base)) % 256
        top = pltpu.roll(surf[0:16, base : base + 256], turn, 1)[:, 0:128]
        low = pltpu.roll(surf[16:32, base : base + 256], turn, 1)[:, 0:128]
        snd[e] = both(top, low).astype(bf16)
    rcv[ens] = snd[ens]

    def deal(step):
        peer = lax.rem(ens + step, members)
        return pltpu.make_async_remote_copy(
            src_ref=snd.at[peer],
            dst_ref=rcv.at[ens],
            send_sem=ens_send.at[step],
            recv_sem=ens_recv.at[ens],
            device_id={"ens": peer},
            device_id_type=MESH,
        )

    for step in range(1, members):
        deal(step).start()
    for step in range(1, members):
        peer = lax.rem(ens + step, members)
        pltpu.make_async_remote_copy(
            src_ref=snd.at[peer],
            dst_ref=rcv.at[peer],
            send_sem=ens_send.at[step],
            recv_sem=ens_recv.at[peer],
            device_id={"ens": peer},
            device_id_type=MESH,
        ).wait_recv()
    got[...] = rcv[...]
    for step in range(1, members):
        deal(step).wait_send()
    for b in range(BLOCKS):

        @pl.when(me < last)
        def _():
            forward(b).wait_send()

        @pl.when(me > 0)
        def _():
            backward(b).wait_send()

    def finish(o, carry):
        pltpu.make_async_copy(xv.at[o], out.at[0, o], out_sem.at[o]).wait()
        return carry

    lax.fori_loop(0, ROWS, finish, 0)


def score_kernel(
    state, got_far, target_far, out, score_far, held, got, target, score, tgt, in_sems, sems, small
):
    ins = [
        pltpu.make_async_copy(got_far, got, small.at[0]),
        pltpu.make_async_copy(target_far, target, small.at[1]),
    ]
    for copy in ins:
        copy.start()
    arrivals = [
        pltpu.make_async_copy(state.at[0, o], held.at[o], in_sems.at[o]) for o in range(ROWS)
    ]
    copies = [pltpu.make_async_copy(held.at[o], out.at[0, o], sems.at[o]) for o in range(ROWS)]
    for arrival in arrivals:
        arrival.start()
    for arrival, copy in zip(arrivals, copies):
        arrival.wait()
        copy.start()
    for copy in ins:
        copy.wait()
    members, cols = got.shape[0], target.shape[2]
    for o in range(ROWS):
        v = target[o]
        tgt[0, o : o + 1, 0:cols] = v[0:1]
        tgt[1, o : o + 1, 0:cols] = v[1:2]
    aim = both(tgt[0], tgt[1])
    field = [got[m].astype(f32) for m in range(members)]
    skill = sum(jnp.abs(f - aim) for f in field) * (1.0 / members)
    spread = jnp.zeros_like(aim)
    for m in range(members):
        for n in range(m):
            spread = spread + jnp.abs(field[m] - field[n])
    fair = skill - spread * (1.0 / (members * (members - 1)))
    other = pltpu.roll(fair, 64, 1)
    for o in range(ROWS):
        score[o, 0:1, :] = fair[o : o + 1, 0:cols]
        score[o, 1:2, :] = other[o : o + 1, 0:cols]
    result = pltpu.make_async_copy(score, score_far, small.at[2])
    result.start()
    result.wait()
    for copy in copies:
        copy.wait()


def body(
    hidden_vectors, target, mix_weight, basis_coef, rescaling_factors,
    up_weight, down_weight, readout_matrix, band_start, band_width,
):
    members = lax.axis_size("ens")
    vmem = pl.BlockSpec(memory_space=pltpu.VMEM)
    smem = pl.BlockSpec(memory_space=pltpu.SMEM)
    basis_coef = basis_coef.transpose(0, 1, 3, 2, 4)
    state, surfaces = pl.pallas_call(
        step_kernel,
        out_shape=(
            jax.ShapeDtypeStruct(hidden_vectors.shape, bf16),
            jax.ShapeDtypeStruct((members, 16, 128), bf16),
        ),
        in_specs=[smem, smem, pl.BlockSpec(memory_space=pl.ANY)] + [vmem] * 6,
        out_specs=(pl.BlockSpec(memory_space=pl.ANY), vmem),
        scratch_shapes=[
            pltpu.VMEM((ROWS, LON, C), bf16),
            pltpu.VMEM((ROWS + 2 * HALO, PAIRS, 4 * C), bf16),
            pltpu.VMEM((ROWS, PAIRS, 2 * C), bf16),
            pltpu.VMEM((ROWS * BMAX, 4 * C, 2 * C), bf16),
            [pltpu.VMEM((752, C), f32)] * 3,
            [pltpu.VMEM((2 * PAIRS, C), f32)] * 3,
            pltpu.VMEM((16 * C, C), f32),
            pltpu.VMEM((SPAN * C, C), f32),
            [pltpu.VMEM((PAIRS, 2 * C), f32)] * 4,
            pltpu.VMEM((192, 256), f32),
            pltpu.VMEM((144, C), f32),
            [pltpu.VMEM((384, C), f32)] * 3,
            [pltpu.VMEM((384, C), f32)] * 3,
            pltpu.VMEM((2 * HALO, LON, C), bf16),
            pltpu.VMEM((2 * HALO, PAIRS, 2 * C), bf16),
            pltpu.VMEM((32, 896), f32),
            pltpu.VMEM((members, 16, 128), bf16),
            pltpu.VMEM((members, 16, 128), bf16),
            pltpu.VMEM((ROWS, 2 * C, C), bf16),
            pltpu.VMEM((PAIRS, C), f32),
            pltpu.SemaphoreType.DMA,
            pltpu.SemaphoreType.DMA((ROWS,)),
            pltpu.SemaphoreType.DMA((2, 2)),
            pltpu.SemaphoreType.DMA((2, 2)),
            pltpu.SemaphoreType.DMA((members,)),
            pltpu.SemaphoreType.DMA((members,)),
        ],
        compiler_params=pltpu.CompilerParams(
            vmem_limit_bytes=56 * 2**20, collective_id=0, has_side_effects=True
        ),
    )(
        band_start, band_width, hidden_vectors, mix_weight, basis_coef,
        rescaling_factors, up_weight, down_weight, readout_matrix,
    )
    target = target.transpose(1, 0, 2)
    state, score = pl.pallas_call(
        score_kernel,
        out_shape=(
            jax.ShapeDtypeStruct(state.shape, bf16),
            jax.ShapeDtypeStruct(target.shape, f32),
        ),
        in_specs=[pl.BlockSpec(memory_space=pl.ANY)] * 3,
        out_specs=[pl.BlockSpec(memory_space=pl.ANY)] * 2,
        scratch_shapes=[
            pltpu.VMEM((ROWS, LON, C), bf16),
            pltpu.VMEM(surfaces.shape, bf16),
            pltpu.VMEM(target.shape, f32),
            pltpu.VMEM(target.shape, f32),
            pltpu.VMEM((2, 16, 128), f32),
            pltpu.SemaphoreType.DMA((ROWS,)),
            pltpu.SemaphoreType.DMA((ROWS,)),
            pltpu.SemaphoreType.DMA((3,)),
        ],
    )(state, surfaces, target)
    return state, score.transpose(1, 0, 2)


def solution(mesh):
    in_specs = (P("ens", "space", None, None), P(None, "space", "ens")) + (P(),) * 8
    out_specs = (P("ens", "space", None, None), P(None, "space", "ens"))
    return jax.shard_map(body, mesh=mesh, in_specs=in_specs, out_specs=out_specs, check_vma=False)
```

```python
import jax
import jax.numpy as jnp
from jax import lax
from jax.experimental import pallas as pl
from jax.experimental.pallas import tpu as pltpu
from jax.sharding import PartitionSpec as P

K = 9
BMAX = 4
HALO = 2
LW = 3
BLOCKS = 2
ROWS = 12
LON = 720
PAIRS = 368
C = 128
STEP = 80
PARTS = ((0, 192), (192, 176))
f32 = jnp.float32
bf16 = jnp.bfloat16
SPAN = 145
MESH = pl.DeviceIdType.MESH


def unit(v, gain):
    return v * lax.rsqrt(jnp.mean(v * v, axis=-1, keepdims=True) + 1e-6) * gain


def prep_row(x, gain, a, s, nrm, raw):
    for t in range(0, LON, STEP):
        v = x[pl.ds(t, STEP), :].astype(f32)
        nrm[pl.ds(8 + t, STEP), :] = unit(v, gain)
        if s is not None:
            raw[pl.ds(t, STEP), :] = v
    nrm[7:8, :] = nrm[727:728, :]
    nrm[728:729, :] = nrm[8:9, :]
    for j in range(4):
        a[:, j * C : (j + 1) * C] = nrm[pl.ds(7 + j, PAIRS, stride=2), :].astype(bf16)
    if s is not None:
        for j in range(2):
            s[:, j * C : (j + 1) * C] = raw[pl.ds(j, PAIRS, stride=2), :].astype(bf16)


def band_rows(b, me, basis, width, cf, bnd):
    lat = jax.lax.broadcasted_iota(jnp.int32, (16, 192), 1)
    own = jax.lax.broadcasted_iota(jnp.int32, (16, 192), 0)
    pick = jnp.where((lat == own + me * ROWS) & (own < ROWS), 1.0, 0.0).astype(bf16)
    row = jax.lax.broadcasted_iota(jnp.int32, (16, 16), 0)
    widths = jnp.zeros((16, 16), jnp.int32)
    for o in range(ROWS):
        widths = jnp.where(row == o, width[me * ROWS + o], widths)
    for k in range(K):
        for l in range(LW):
            v = basis[b, k, l].astype(f32)
            for q in range(BMAX):
                at = (q * LW + l) * 16 + k
                cf[at : at + 1, 0:192] = v[q : q + 1]
    for q in range(BMAX):
        for l in range(LW):
            at = q * LW + l
            part = lax.dot_general(
                pick,
                cf[at * 16 : at * 16 + 16, 0:192].astype(bf16),
                (((1,), (1,)), ((), ())),
                preferred_element_type=f32,
            )
            part = jnp.where(widths > q, part, 0.0)
            bnd[at * ROWS : at * ROWS + ROWS, 0:16] = part[:ROWS]


def spread_mix(b, mix, mx):
    for k in range(K):
        mx[pl.ds(k, C, stride=16), :] = mix[b, k].astype(f32)


def channels(coef, mx, wf, low, count):
    for u in range(count):
        c = low + u
        rhs = jnp.concatenate(
            [mx[pl.ds(c * 32, 16), :], mx[pl.ds(c * 32 + 16, 16), :]], axis=1
        ).astype(bf16)
        out = jnp.dot(coef, rhs, preferred_element_type=f32)
        wf[pl.ds(c * 2 * SPAN, 144), :] = out[:, :C]
        wf[pl.ds(c * 2 * SPAN + SPAN, 144), :] = out[:, C:]


def place(o, wf, taps):
    for q in range(BMAX):
        i = o * BMAX + q
        for l in range(LW):
            w = wf[pl.ds((q * LW + l) * ROWS + o, C, stride=SPAN), :].astype(bf16)
            taps[i, l * C : (l + 1) * C, 0:C] = w
            taps[i, (l + 1) * C : (l + 2) * C, C : 2 * C] = w


def taps_beside(prepare, bnd, mx, wf, taps):
    coef = bnd[0:144, 0:16].astype(bf16)

    def some(i, carry):
        for k in range(3):
            prepare(3 * i + k, k)
        channels(coef, mx, wf, i * 16, 16)
        return carry

    def put(o, carry):
        place(o, wf, taps)
        return carry

    lax.fori_loop(0, 4, some, 0)
    lax.fori_loop(0, ROWS, put, 0)


def prep_pairs(s, gain, a, even, odd):
    for p, n in PARTS:
        e = unit(s[pl.ds(p, n), 0:C].astype(f32), gain)
        o = unit(s[pl.ds(p, n), C : 2 * C].astype(f32), gain)
        a[pl.ds(p, n), C : 2 * C] = e.astype(bf16)
        a[pl.ds(p, n), 2 * C : 3 * C] = o.astype(bf16)
        even[pl.ds(8 + p, n), :] = e
        odd[pl.ds(8 + p, n), :] = o
    odd[7:8, :] = odd[367:368, :]
    even[368:369, :] = even[8:9, :]
    a[:, 0:C] = odd[7 : 7 + PAIRS, :].astype(bf16)
    a[:, 3 * C : 4 * C] = even[9 : 9 + PAIRS, :].astype(bf16)


def conv_row(o, start, first, a, s, taps, car):
    base = start[first + o] - first + HALO
    rows = [jnp.clip(base + q, 0, ROWS + 2 * HALO - 1) for q in range(BMAX)]
    for p, n in PARTS:
        acc = jnp.dot(a[rows[0], pl.ds(p, n), :], taps[o * BMAX], preferred_element_type=f32)
        for q in range(1, BMAX):
            acc += jnp.dot(
                a[rows[q], pl.ds(p, n), :], taps[o * BMAX + q], preferred_element_type=f32
            )
        car[pl.ds(p, n), :] = (s[o, pl.ds(p, n), :].astype(f32) + acc).astype(bf16).astype(f32)


def mlp_row(gain, up, down, car, emit):
    for p, n in PARTS:
        rest = jnp.concatenate([car[pl.ds(p, n), :C], car[pl.ds(p, n), C:]], axis=0)
        h = jnp.dot(unit(rest, gain).astype(bf16), up, preferred_element_type=f32)
        h = (0.5 * h * (1.0 + lax.erf(h * 0.7071067811865476))).astype(bf16)
        y = rest + jnp.dot(h, down, preferred_element_type=f32)
        emit(p, n, y[:n], y[n:])


def both(first, second):
    lane = jax.lax.broadcasted_iota(jnp.int32, first.shape, 1)
    return jnp.where(lane < 64, first, pltpu.roll(second, 64, 1))


def step_kernel(
    start, width, x, mix, basis, gains, up, down, readout,
    out, got,
    xv, a, s, taps, nrms, fins, mx, wf, cars, cf, bnd, evens, odds,
    halo0, halo1, surf, snd, rcv, leads, seen,
    x_sem, out_sem, send_sem, recv_sem, ens_send, ens_recv,
):
    me = lax.axis_index("space")
    ens = lax.axis_index("ens")
    members = rcv.shape[0]
    last = lax.axis_size("space") - 1
    barrier = pltpu.get_barrier_semaphore()
    for step in range(1, members):
        pl.semaphore_signal(
            barrier, inc=1, device_id={"ens": lax.rem(ens + step, members)}, device_id_type=MESH
        )

    @pl.when(me > 0)
    def _():
        pl.semaphore_signal(barrier, inc=1, device_id={"space": me - 1}, device_id_type=MESH)

    @pl.when(me < last)
    def _():
        pl.semaphore_signal(barrier, inc=1, device_id={"space": me + 1}, device_id_type=MESH)

    x_copy = pltpu.make_async_copy(x.at[0], xv, x_sem)
    x_copy.start()
    mx[...] = jnp.zeros_like(mx)
    cf[...] = jnp.zeros_like(cf)

    def clear(i, carry):
        taps[i, 3 * C : 4 * C, 0:C] = jnp.zeros((C, C), bf16)
        taps[i, 0:C, C : 2 * C] = jnp.zeros((C, C), bf16)
        return carry

    lax.fori_loop(0, ROWS * BMAX, clear, 0)
    for i in range(HALO):
        a[i] = jnp.zeros((PAIRS, 4 * C), bf16)
        a[ROWS + HALO + i] = jnp.zeros((PAIRS, 4 * C), bf16)
    band_rows(0, me, basis, width, cf, bnd)
    spread_mix(0, mix, mx)

    turned = jnp.concatenate([readout[...].astype(f32), jnp.zeros((C - 2, C), f32)], axis=0).T
    seen_lane = jax.lax.broadcasted_iota(jnp.int32, (C, C), 1)
    for o in range(ROWS):
        for side in range(2):
            at = 32 * side + o
            lead = jnp.where(seen_lane == at, turned[:, 0:1], 0.0)
            lead = jnp.where(seen_lane == at + 16, turned[:, 1:2], lead)
            leads[o, side * C : (side + 1) * C, :] = lead.astype(bf16)
    seen[...] = jnp.zeros_like(seen)
    middle = (me > 0) & (me < last)

    @pl.when(middle)
    def _():
        pl.semaphore_wait(barrier, members + 1)

    @pl.when(jnp.logical_not(middle))
    def _():
        pl.semaphore_wait(barrier, members)

    def forward(b):
        source, landing = (x.at[0], halo0) if b == 0 else (s, halo1)
        return pltpu.make_async_remote_copy(
            src_ref=source.at[pl.ds(ROWS - HALO, HALO)],
            dst_ref=landing.at[pl.ds(0, HALO)],
            send_sem=send_sem.at[b, 0],
            recv_sem=recv_sem.at[b, 0],
            device_id={"space": me + 1},
            device_id_type=MESH,
        )

    def backward(b):
        source, landing = (x.at[0], halo0) if b == 0 else (s, halo1)
        return pltpu.make_async_remote_copy(
            src_ref=source.at[pl.ds(0, HALO)],
            dst_ref=landing.at[pl.ds(HALO, HALO)],
            send_sem=send_sem.at[b, 1],
            recv_sem=recv_sem.at[b, 1],
            device_id={"space": me - 1},
            device_id_type=MESH,
        )

    def send_forward(b):
        @pl.when(me < last)
        def _():
            forward(b).start()

    def send_backward(b):
        @pl.when(me > 0)
        def _():
            backward(b).start()

    send_forward(0)
    send_backward(0)
    first = me * ROWS

    def halo_rows(b, side):
        def fill():
            for i in range(HALO):
                at = side * HALO + i
                row = a.at[side * (ROWS + HALO) + i]
                if b == 0:
                    prep_row(halo0.at[at], gains[0, 0:1], row, None, nrms[i], None)
                else:
                    prep_pairs(halo1.at[at], gains[1, 0:1], row, evens[i], odds[i])

        def empty():
            for i in range(HALO):
                a[side * (ROWS + HALO) + i] = jnp.zeros((PAIRS, 4 * C), bf16)

        has = me > 0 if side == 0 else me < last

        @pl.when(has)
        def _():
            (forward(b) if side == 0 else backward(b)).wait_recv()
            fill()

        @pl.when(jnp.logical_not(has))
        def _():
            empty()


    def rows(b, group):
        gain2 = gains[b, 1:2]
        up_matrix, down_matrix = up[b], down[b]
        for o, car in zip(group, cars):
            conv_row(o, start, first, a, s, taps, car)
        for i, (o, car) in enumerate(zip(group, cars)):
            fin = fins[i % 2]

            def emit(p, n, e, d):
                if b == 0:
                    s[o, pl.ds(p, n), 0:C] = e.astype(bf16)
                    s[o, pl.ds(p, n), C : 2 * C] = d.astype(bf16)
                else:
                    fin[pl.ds(2 * p, n, stride=2), :] = e
                    fin[pl.ds(2 * p + 1, n, stride=2), :] = d
                    pair = jnp.concatenate([e.astype(bf16), d.astype(bf16)], axis=1)
                    seen[pl.ds(p, n), :] += jnp.dot(
                        pair, leads[o], preferred_element_type=f32
                    )

            mlp_row(gain2, up_matrix, down_matrix, car, emit)
            if b == 1:
                xv[o] = fin[0:LON, :].astype(bf16)
                pltpu.make_async_copy(xv.at[o], out.at[0, o], out_sem.at[o]).start()

    def inner_rows(b):
        rows(b, list(range(HALO, ROWS - HALO)))

    def outer_rows(b):
        halo_rows(b, 0)
        halo_rows(b, 1)
        rows(b, [0, 1, ROWS - 2, ROWS - 1])

    x_copy.wait()

    def prep0(o, k):
        prep_row(xv.at[o], gains[0, 0:1], a.at[o + HALO], s.at[o], nrms[k], fins[k])

    taps_beside(prep0, bnd, mx, wf, taps)
    inner_rows(0)
    outer_rows(0)
    send_backward(1)
    send_forward(1)

    band_rows(1, me, basis, width, cf, bnd)
    spread_mix(1, mix, mx)

    def prep1(o, k):
        prep_pairs(s.at[o], gains[1, 0:1], a.at[o + HALO], evens[k], odds[k])

    taps_beside(prep1, bnd, mx, wf, taps)
    inner_rows(1)
    outer_rows(1)

    fin = fins[0]
    fin[pl.ds(0, PAIRS, stride=2), :] = seen[...]
    fin[pl.ds(1, PAIRS, stride=2), :] = pltpu.roll(seen[...], C - 32, 1)
    for t in range(0, 640, C):
        surf[:, t : t + C] = fin[t : t + C, :].T[0:32]
    surf[:, 640:736] = fin[640:736, :].T[0:32]
    cols = LON // members
    for e in range(members):
        base = e * cols // 128 * 128
        turn = (256 - (e * cols - base)) % 256
        top = pltpu.roll(surf[0:16, base : base + 256], turn, 1)[:, 0:128]
        low = pltpu.roll(surf[16:32, base : base + 256], turn, 1)[:, 0:128]
        snd[e] = both(top, low).astype(bf16)
    rcv[ens] = snd[ens]

    def deal(step):
        peer = lax.rem(ens + step, members)
        return pltpu.make_async_remote_copy(
            src_ref=snd.at[peer],
            dst_ref=rcv.at[ens],
            send_sem=ens_send.at[step],
            recv_sem=ens_recv.at[ens],
            device_id={"ens": peer},
            device_id_type=MESH,
        )

    for step in range(1, members):
        deal(step).start()
    for step in range(1, members):
        peer = lax.rem(ens + step, members)
        pltpu.make_async_remote_copy(
            src_ref=snd.at[peer],
            dst_ref=rcv.at[peer],
            send_sem=ens_send.at[step],
            recv_sem=ens_recv.at[peer],
            device_id={"ens": peer},
            device_id_type=MESH,
        ).wait_recv()
    got[...] = rcv[...]
    for step in range(1, members):
        deal(step).wait_send()
    for b in range(BLOCKS):

        @pl.when(me < last)
        def _():
            forward(b).wait_send()

        @pl.when(me > 0)
        def _():
            backward(b).wait_send()

    def finish(o, carry):
        pltpu.make_async_copy(xv.at[o], out.at[0, o], out_sem.at[o]).wait()
        return carry

    lax.fori_loop(0, ROWS, finish, 0)


def score_kernel(
    state, got_far, target_far, out, score_far, held, got, target, score, tgt, in_sems, sems, small
):
    ins = [
        pltpu.make_async_copy(got_far, got, small.at[0]),
        pltpu.make_async_copy(target_far, target, small.at[1]),
    ]
    for copy in ins:
        copy.start()
    arrivals = [
        pltpu.make_async_copy(state.at[0, o], held.at[o], in_sems.at[o]) for o in range(ROWS)
    ]
    copies = [pltpu.make_async_copy(held.at[o], out.at[0, o], sems.at[o]) for o in range(ROWS)]
    for arrival in arrivals:
        arrival.start()
    for arrival, copy in zip(arrivals, copies):
        arrival.wait()
        copy.start()
    for copy in ins:
        copy.wait()
    members, cols = got.shape[0], target.shape[2]
    for o in range(ROWS):
        v = target[o]
        tgt[0, o : o + 1, 0:cols] = v[0:1]
        tgt[1, o : o + 1, 0:cols] = v[1:2]
    aim = both(tgt[0], tgt[1])
    field = [got[m].astype(f32) for m in range(members)]
    skill = sum(jnp.abs(f - aim) for f in field) * (1.0 / members)
    spread = jnp.zeros_like(aim)
    for m in range(members):
        for n in range(m):
            spread = spread + jnp.abs(field[m] - field[n])
    fair = skill - spread * (1.0 / (members * (members - 1)))
    other = pltpu.roll(fair, 64, 1)
    for o in range(ROWS):
        score[o, 0:1, :] = fair[o : o + 1, 0:cols]
        score[o, 1:2, :] = other[o : o + 1, 0:cols]
    result = pltpu.make_async_copy(score, score_far, small.at[2])
    result.start()
    result.wait()
    for copy in copies:
        copy.wait()


def body(
    hidden_vectors, target, mix_weight, basis_coef, rescaling_factors,
    up_weight, down_weight, readout_matrix, band_start, band_width,
):
    members = lax.axis_size("ens")
    vmem = pl.BlockSpec(memory_space=pltpu.VMEM)
    smem = pl.BlockSpec(memory_space=pltpu.SMEM)
    basis_coef = basis_coef.transpose(0, 1, 3, 2, 4)
    state, surfaces = pl.pallas_call(
        step_kernel,
        out_shape=(
            jax.ShapeDtypeStruct(hidden_vectors.shape, bf16),
            jax.ShapeDtypeStruct((members, 16, 128), bf16),
        ),
        in_specs=[smem, smem, pl.BlockSpec(memory_space=pl.ANY)] + [vmem] * 6,
        out_specs=(pl.BlockSpec(memory_space=pl.ANY), vmem),
        scratch_shapes=[
            pltpu.VMEM((ROWS, LON, C), bf16),
            pltpu.VMEM((ROWS + 2 * HALO, PAIRS, 4 * C), bf16),
            pltpu.VMEM((ROWS, PAIRS, 2 * C), bf16),
            pltpu.VMEM((ROWS * BMAX, 4 * C, 2 * C), bf16),
            [pltpu.VMEM((752, C), f32)] * 3,
            [pltpu.VMEM((2 * PAIRS, C), f32)] * 3,
            pltpu.VMEM((16 * C, C), f32),
            pltpu.VMEM((SPAN * C, C), f32),
            [pltpu.VMEM((PAIRS, 2 * C), f32)] * 8,
            pltpu.VMEM((192, 256), f32),
            pltpu.VMEM((144, C), f32),
            [pltpu.VMEM((384, C), f32)] * 3,
            [pltpu.VMEM((384, C), f32)] * 3,
            pltpu.VMEM((2 * HALO, LON, C), bf16),
            pltpu.VMEM((2 * HALO, PAIRS, 2 * C), bf16),
            pltpu.VMEM((32, 896), f32),
            pltpu.VMEM((members, 16, 128), bf16),
            pltpu.VMEM((members, 16, 128), bf16),
            pltpu.VMEM((ROWS, 2 * C, C), bf16),
            pltpu.VMEM((PAIRS, C), f32),
            pltpu.SemaphoreType.DMA,
            pltpu.SemaphoreType.DMA((ROWS,)),
            pltpu.SemaphoreType.DMA((2, 2)),
            pltpu.SemaphoreType.DMA((2, 2)),
            pltpu.SemaphoreType.DMA((members,)),
            pltpu.SemaphoreType.DMA((members,)),
        ],
        compiler_params=pltpu.CompilerParams(
            vmem_limit_bytes=56 * 2**20, collective_id=0, has_side_effects=True
        ),
    )(
        band_start, band_width, hidden_vectors, mix_weight, basis_coef,
        rescaling_factors, up_weight, down_weight, readout_matrix,
    )
    target = target.transpose(1, 0, 2)
    state, score = pl.pallas_call(
        score_kernel,
        out_shape=(
            jax.ShapeDtypeStruct(state.shape, bf16),
            jax.ShapeDtypeStruct(target.shape, f32),
        ),
        in_specs=[pl.BlockSpec(memory_space=pl.ANY)] * 3,
        out_specs=[pl.BlockSpec(memory_space=pl.ANY)] * 2,
        scratch_shapes=[
            pltpu.VMEM((ROWS, LON, C), bf16),
            pltpu.VMEM(surfaces.shape, bf16),
            pltpu.VMEM(target.shape, f32),
            pltpu.VMEM(target.shape, f32),
            pltpu.VMEM((2, 16, 128), f32),
            pltpu.SemaphoreType.DMA((ROWS,)),
            pltpu.SemaphoreType.DMA((ROWS,)),
            pltpu.SemaphoreType.DMA((3,)),
        ],
    )(state, surfaces, target)
    return state, score.transpose(1, 0, 2)


def solution(mesh):
    in_specs = (P("ens", "space", None, None), P(None, "space", "ens")) + (P(),) * 8
    out_specs = (P("ens", "space", None, None), P(None, "space", "ens"))
    return jax.shard_map(body, mesh=mesh, in_specs=in_specs, out_specs=out_specs, check_vma=False)
```
